32 devices in a mesh: dp: 2 (over x), row: 4 (over y, core), col: 4 (over z).
Axes of the slice: x: 2, y: 2, z: 4, core: 2. Of those that a mesh axis runs over, the one named last changes fastest.
Arguments:
- tokens: bfloat16 [8192, 1024], P(('dp', 'col'), 'row'), may hold values from -40 to 40
- segments: int32 [8, 1024], P(('dp', 'row')), may hold values from 0 to 3, never falling along the last dimension, each value on 1 to 768 neighbouring positions
- cotangent: bfloat16 [8192, 1024], P(('dp', 'col'), 'row'), may hold values from -6 to 6
- norm_in: float32 [1024], P('row'), may hold values from 0.5 to 1.5
- w_gate_ssm: bfloat16 [1024, 1536], P('row', 'col'), may hold values from -0.1875 to 0.1875
- w_conv_in: bfloat16 [1024, 1536], P('row', 'col'), may hold values from -0.5 to 0.5
- w_step: bfloat16 [1024, 24], P('row', 'col'), may hold values from -0.1875 to 0.1875
- w_query: bfloat16 [1024, 512], P('row', 'col'), may hold values from -0.1875 to 0.1875
- w_shared: bfloat16 [1024, 512], P('row', 'col'), may hold values from -0.1875 to 0.1875
- conv_main: float32 [5, 1536], P(None, 'col'), may hold values from -0.5 to 0.5
- conv_side: float32 [5, 256], replicated, may hold values from -0.5 to 0.5
- step_bias: float32 [24], P('col'), may hold values from -5 to -1
- decay_log: float32 [24], P('col'), may hold values from -1 to 2
- skip_gain: float32 [24], P('col'), may hold values from 0.25 to 1.75
- norm_ssm: float32 [1536], P('col'), may hold values from 0.5 to 1.5
- w_ssm_out: bfloat16 [1536, 1024], P('col', 'row'), may hold values from -0.15625 to 0.15625
- w_att_out: bfloat16 [512, 1024], P('col', 'row'), may hold values from -1 to 1
- norm_mlp: float32 [1024], P('row'), may hold values from 0.5 to 1.5
- w_gate: bfloat16 [1024, 2048], P('row', 'col'), may hold values from -0.1875 to 0.1875
- w_up: bfloat16 [1024, 2048], P('row', 'col'), may hold values from -0.1875 to 0.1875
- w_down: bfloat16 [2048, 1024], P('col', 'row'), may hold values from -0.1875 to 0.1875
Outputs:
- block_out: bfloat16 [8192, 1024], P(('dp', 'col'), 'row')
- grad_tokens: float32 [8192, 1024], P(('dp', 'col'), 'row')
- grad_norm_in: float32 [1024], P('row')
- grad_gate_ssm: float32 [1024, 1536], P('row', 'col')
- grad_conv_in: float32 [1024, 1536], P('row', 'col')
- grad_step: float32 [1024, 24], P('row', 'col')
- grad_query: float32 [1024, 512], P('row', 'col')
- grad_shared: float32 [1024, 512], P('row', 'col')
- grad_conv_main: float32 [5, 1536], P(None, 'col')
- grad_conv_side: float32 [5, 256], replicated
- grad_step_bias: float32 [24], P('col')
- grad_decay_log: float32 [24], P('col')
- grad_skip_gain: float32 [24], P('col')
- grad_norm_ssm: float32 [1536], P('col')
- grad_ssm_out: float32 [1536, 1024], P('col', 'row')
- grad_att_out: float32 [512, 1024], P('col', 'row')
- grad_norm_mlp: float32 [1024], P('row')
- grad_gate: float32 [1024, 2048], P('row', 'col')
- grad_up: float32 [1024, 2048], P('row', 'col')
- grad_down: float32 [2048, 1024], P('col', 'row')
The draws below stay inside these ranges and needn't reach their ends.
Inputs may be any that keep to these rules, and one draw needn't show every extreme that they name: `segments`: within a sequence document numbers never fall and start at 0; each document covers 1 to 768 positions, one of them exactly that many.
All inputs are finite; a program needn't handle non-finite values.
Results may differ from the reference program's by a relative error of at most 0.013.
Values may be sent and summed in bfloat16 or wider, within the bound.
No kernel may reach another device: no remote copies, remote signals or barrier semaphores. Data moves between devices by JAX's collectives and lax.ppermute only.
A program may use at most 128 MiB of HBM per device.

```python
import math
import jax
import jax.numpy as jnp
import numpy as np
from jax import lax

D = 1024
HEADS = 24
STATE = 128
CONV = 4
KVH = 2
HD = 64
FF = 2048
LENGTH = 1024
DSSM = 1536
QD = 512
SHARED = 512
SEQUENCES = 8
TOKENS = 8192


def draw_tokens(key, part):
    key = jax.random.fold_in(key, 11)
    first_key, second_key, third_key = jax.random.split(key, 3)
    rising = 3.0 ** (jnp.arange(D).astype(jnp.float32) / D)
    rough = jax.random.uniform(second_key, (D,), jnp.float32, 0.7, 1.4)
    base = jax.random.normal(first_key, (TOKENS, D), jnp.float32)
    row_scales = jnp.exp(jax.random.uniform(third_key, (TOKENS, 1), jnp.float32, -0.7, 0.7))
    return jnp.clip(base * row_scales * rising[None, :] * rough[None, :], -40.0, 40.0).astype(jnp.bfloat16)


def draw_w_conv_in(key, part):
    key = jax.random.fold_in(key, 12)
    base = jax.random.normal(key, (D, DSSM), jnp.float32) * D ** (-0.5)
    rising = 3.0 ** (jnp.arange(DSSM).astype(jnp.float32) / DSSM)
    return jnp.clip(base * rising[None, :] * 0.6, -0.5, 0.5).astype(jnp.bfloat16)


def steps_of(key, extent, cuts, least, high):
    def one(dim, blocks):
        steps = jax.random.uniform(jax.random.fold_in(jax.random.fold_in(key, 6), dim), (blocks,), jnp.float32, least / len(cuts), high / len(cuts))
        return jnp.repeat(jnp.exp(steps), extent[dim] // blocks).reshape((-1,) + (1,) * (len(extent) - dim - 1))

    factor_of = one(*cuts[0])
    for cut in cuts[1:]:
        factor_of = factor_of * one(*cut)
    return factor_of


def length_profile(amount, total, most, skew):
    weights = [(1 << 20) // math.isqrt(standing ** skew) + 1 for standing in range(2, amount + 1)]
    rest, counts = total - most - (amount - 1), [1] * (amount - 1)
    while rest > 0:
        free = [i for i in range(amount - 1) if counts[i] < most]
        whole, left = sum([weights[i] for i in free]), rest
        for i in free:
            more = min(most - counts[i], max(1, left * weights[i] // whole), rest)
            counts[i] = counts[i] + more
            rest = rest - more
    return np.array([most] + counts)


def uneven(own_key, number_of, total, limit, slope):
    if number_of == 2:
        one = jax.random.randint(own_key, (), max(1, total - limit), min(limit, total - 1) + 1)
        return jnp.stack([one, total - one])
    tallies = jnp.asarray(length_profile(number_of, total, limit, slope), jnp.int32)
    couples = (number_of - 1) // 2
    donor, taker = tallies[1:1 + 2 * couples:2], tallies[2:2 + 2 * couples:2]
    margin = jnp.minimum(donor - 1, limit - taker)
    moved = jax.random.randint(jax.random.fold_in(own_key, 1), (couples,), 0, 1 << 20) % (margin + 1)
    tallies = tallies.at[1:1 + 2 * couples:2].set(donor - moved).at[2:2 + 2 * couples:2].set(taker + moved)
    return tallies[jax.random.permutation(jax.random.fold_in(own_key, 2), number_of)]


def scatter_about(stream_key, shape, spread, limit, pieces=(), kind=jnp.bfloat16):
    factor_of = steps_of(stream_key, shape, pieces, -0.22, 0.18) if pieces else 1.0
    values = jax.random.normal(stream_key, shape, jnp.float32) * spread * factor_of
    return jnp.minimum(jnp.maximum(values, -limit), limit).astype(kind)


def setup_inputs(seed: int = 0) -> dict:
    key_of = jax.random.split(jax.random.key(seed), 22)
    return {
        "tokens": draw_tokens(jax.random.fold_in(key_of[21], 71), 0),
        "segments": jax.vmap(lambda own: jnp.searchsorted(jnp.cumsum(uneven(own, 4, LENGTH, LENGTH * 3 // 4, 1)), jnp.arange(LENGTH), side="right"))(jax.random.split(key_of[1], SEQUENCES)).reshape((SEQUENCES, LENGTH)).astype(jnp.int32),
        "cotangent": scatter_about(key_of[2], (TOKENS, D), 1.0, 6.0, ((0, 8), (1, 4))),
        "norm_in": jnp.clip(1.0 + 0.1 * jax.random.normal(key_of[3], (D,), jnp.float32), 0.5, 1.5),
        "w_gate_ssm": scatter_about(key_of[4], (D, DSSM), D ** -0.5, 0.1875, ((0, 4), (1, 4))),
        "w_conv_in": draw_w_conv_in(jax.random.fold_in(key_of[21], 71), 0),
        "w_step": scatter_about(key_of[6], (D, HEADS), D ** -0.5, 0.1875, ((0, 4), (1, 4))),
        "w_query": scatter_about(key_of[7], (D, QD), D ** -0.5, 0.1875, ((0, 4), (1, 4))),
        "w_shared": scatter_about(key_of[8], (D, SHARED), D ** -0.5, 0.1875, ((0, 4), (1, 4))),
        "conv_main": jnp.clip(jax.random.uniform(key_of[9], (CONV + 1, DSSM), jnp.float32, -0.5, 0.5) * steps_of(key_of[9], (CONV + 1, DSSM), ((1, 4),), -0.4, 0.0), -0.5, 0.5),
        "conv_side": jnp.clip(jax.random.uniform(key_of[10], (CONV + 1, 2 * STATE), jnp.float32, -0.5, 0.5), -0.5, 0.5),
        "step_bias": jnp.clip(-5.0 + 4.0 * jax.random.uniform(key_of[11], (HEADS,), jnp.float32) ** steps_of(key_of[11], (HEADS,), ((0, 4),), -0.2, 0.2), -5.0, -1.0),
        "decay_log": jnp.clip(-1.0 + 3.0 * jax.random.uniform(key_of[12], (HEADS,), jnp.float32) ** steps_of(key_of[12], (HEADS,), ((0, 4),), -0.2, 0.2), -1.0, 2.0),
        "skip_gain": jnp.clip(1.0 + 0.15 * jax.random.normal(key_of[13], (HEADS,), jnp.float32), 0.25, 1.75),
        "norm_ssm": jnp.clip(1.0 + 0.1 * jax.random.normal(key_of[14], (DSSM,), jnp.float32), 0.5, 1.5),
        "w_ssm_out": scatter_about(key_of[15], (DSSM, D), DSSM ** -0.5, 0.15625, ((0, 4), (1, 4))),
        "w_att_out": scatter_about(key_of[16], (QD, D), (QD // 16) ** -0.5, 1.0, ((0, 4), (1, 4))),
        "norm_mlp": jnp.clip(1.0 + 0.1 * jax.random.normal(key_of[17], (D,), jnp.float32), 0.5, 1.5),
        "w_gate": scatter_about(key_of[18], (D, FF), D ** -0.5, 0.1875, ((0, 4), (1, 4))),
        "w_up": scatter_about(key_of[19], (D, FF), D ** -0.5, 0.1875, ((0, 4), (1, 4))),
        "w_down": scatter_about(key_of[20], (FF, D), (FF // 2) ** -0.5, 0.1875, ((0, 4), (1, 4))),
    }


norm_eps = 1e-05
rope_theta = 10000.0
exact_mode = lax.Precision.HIGHEST

@jax.custom_vjp
def low(v):
    return lax.optimization_barrier(v.astype(jnp.bfloat16)).astype(jnp.float32)

@jax.custom_vjp
def low_back(v):
    return v

def low_keep(v):
    return (low(v), None)

def low_pass(kept, grad):
    return (grad,)

def back_keep(v):
    return (v, None)

def back_low(kept, grad):
    return (low(grad),)
low.defvjp(low_keep, low_pass)
low_back.defvjp(back_keep, back_low)

def rotate_pairs(values, places):
    half_width = values.shape[-1] // 2
    powers = jnp.arange(half_width).astype(jnp.float32) * (2.0 / values.shape[-1])
    angles = places[:, None] * (rope_theta ** (-powers))[None, :]
    cosine = jnp.cos(angles)[:, None, :]
    sine_part = jnp.sin(angles)[:, None, :]
    first_half = values[..., :half_width]
    second = values[..., half_width:]
    return jnp.concatenate([first_half * cosine - second * sine_part, second * cosine + first_half * sine_part], axis=-1)

def causal_conv(signal, conv_taps, segment):
    tap_count = conv_taps.shape[0] - 1
    seq_length = signal.shape[0]
    result = jnp.zeros_like(signal) + conv_taps[tap_count][None, :]
    for offset in range(tap_count):
        shifted = jnp.pad(signal, ((offset, 0), (0, 0)))[:seq_length]
        earlier = jnp.pad(segment, (offset, 0), constant_values=-1)[:seq_length]
        same_doc = (earlier == segment).astype(signal.dtype)
        result = result + conv_taps[tap_count - 1 - offset][None, :] * shifted * same_doc[:, None]
    return jax.nn.silu(result)

def mixer_core(gate_in, conv_in, step_in, query_in, state_b, state_c, key_in, value_in, segment, conv_main, conv_side, step_bias, decay_log, skip_gain):
    seq_length = gate_in.shape[0]
    head_count = step_in.shape[1]
    channels = conv_in.shape[1]
    state_width = state_b.shape[1]
    convolved = causal_conv(jnp.concatenate([conv_in, state_b, state_c], axis=1), jnp.concatenate([conv_main, conv_side], axis=1), segment)
    inner_path = convolved[:, :channels]
    input_b = low(convolved[:, channels:channels + state_width])
    input_c = low(convolved[:, channels + state_width:])
    step_size = jax.nn.softplus(step_in + step_bias[None, :])
    decay_sum = jnp.cumsum(step_size * (-jnp.exp(decay_log))[None, :], axis=0)
    places = jnp.arange(seq_length)
    allowed = (places[:, None] >= places[None, :]) & (segment[:, None] == segment[None, :])
    intersection = low_back(jnp.dot(input_c, input_b.T, precision=exact_mode))
    decay_gap = jnp.minimum(decay_sum.T[:, :, None] - decay_sum.T[:, None, :], 0.0)
    mixing = low(jnp.where(allowed[None], jnp.exp(decay_gap), 0.0) * step_size.T[:, None, :] * intersection[None])
    heads_in = inner_path.reshape(seq_length, head_count, -1)
    scanned = low_back(jnp.einsum('hij,jhp->ihp', mixing, low(heads_in), precision=exact_mode))
    gated_out = (scanned + skip_gain[None, :, None] * heads_in).reshape(seq_length, channels) * jax.nn.silu(gate_in)
    places_float = places.astype(jnp.float32)
    query_heads = low(rotate_pairs(query_in.reshape(seq_length, -1, HD), places_float))
    key_heads = low(rotate_pairs(key_in.reshape(seq_length, -1, HD), places_float))
    value_heads = low(value_in.reshape(seq_length, -1, HD))
    group_size = query_heads.shape[1] // key_heads.shape[1]
    key_heads = jnp.repeat(key_heads, group_size, axis=1)
    value_heads = jnp.repeat(value_heads, group_size, axis=1)
    scores = jnp.einsum('ihd,jhd->hij', query_heads, key_heads, precision=exact_mode) * HD ** (-0.5)
    scores = low_back(jnp.where(allowed[None], scores, -1000000000.0))
    row_top = lax.optimization_barrier(jnp.max(scores, axis=2, keepdims=True))
    exponents = jnp.exp(scores - row_top)
    softmax_out = low(exponents / lax.optimization_barrier(jnp.sum(exponents, axis=2, keepdims=True)))
    attended = jnp.einsum('hij,jhd->ihd', softmax_out, value_heads, precision=exact_mode).reshape(seq_length, -1)
    return (gated_out, low(low_back(attended)))

def rms_scale(values, gain):
    return values * lax.rsqrt(lax.optimization_barrier(jnp.mean(values * values, axis=-1, keepdims=True)) + norm_eps) * gain

def product(left, right):
    return jnp.dot(left, right, precision=exact_mode)

def reference(tokens, segments, cotangent, norm_in, w_gate_ssm, w_conv_in, w_step, w_query, w_shared, conv_main, conv_side, step_bias, decay_log, skip_gain, norm_ssm, w_ssm_out, w_att_out, norm_mlp, w_gate, w_up, w_down):

    def forward(tokens_in, norm_in, w_gate_ssm, w_conv_in, w_step, w_query, w_shared, conv_main, conv_side, step_bias, decay_log, skip_gain, norm_ssm, w_ssm_out, w_att_out, norm_mlp, w_gate, w_up, w_down):
        hidden_in = low(rms_scale(tokens_in, norm_in))
        gate_all = low_back(product(hidden_in, w_gate_ssm))
        conv_all = low_back(product(hidden_in, w_conv_in))
        step_all = low_back(product(hidden_in, w_step))
        query_all = low_back(product(hidden_in, w_query))
        shared_all = low(low_back(product(hidden_in, w_shared)))
        key_start = 2 * STATE
        value_start = 2 * STATE + KVH * HD

        def one_sequence(seq_items):
            shared_seq = seq_items[4]
            return mixer_core(seq_items[0], seq_items[1], seq_items[2], seq_items[3], shared_seq[:, :STATE], shared_seq[:, STATE:key_start], shared_seq[:, key_start:value_start], shared_seq[:, value_start:], seq_items[5], conv_main, conv_side, step_bias, decay_log, skip_gain)
        stacked = tuple((array_piece.reshape(SEQUENCES, LENGTH, -1) for array_piece in (gate_all, conv_all, step_all, query_all, shared_all)))
        gated_all, attended_all = lax.map(jax.checkpoint(one_sequence), stacked + (segments,))
        gated_all = gated_all.reshape(TOKENS, -1)
        attended_all = attended_all.reshape(TOKENS, -1)
        normed = low(rms_scale(gated_all, norm_ssm))
        mixed = tokens_in + low_back(product(normed, w_ssm_out)) + low_back(product(attended_all, w_att_out))
        hidden_mlp = low(rms_scale(mixed, norm_mlp))
        gate_proj = low_back(product(hidden_mlp, w_gate))
        up_proj = low_back(product(hidden_mlp, w_up))
        inner_mlp = low(jax.nn.silu(gate_proj) * up_proj)
        return mixed + low_back(product(inner_mlp, w_down))
    result, pullback = jax.vjp(forward, tokens.astype(jnp.float32), norm_in, w_gate_ssm.astype(jnp.float32), w_conv_in.astype(jnp.float32), w_step.astype(jnp.float32), w_query.astype(jnp.float32), w_shared.astype(jnp.float32), conv_main, conv_side, step_bias, decay_log, skip_gain, norm_ssm, w_ssm_out.astype(jnp.float32), w_att_out.astype(jnp.float32), norm_mlp, w_gate.astype(jnp.float32), w_up.astype(jnp.float32), w_down.astype(jnp.float32))
    grads = pullback(cotangent.astype(jnp.float32))
    return (result.astype(jnp.bfloat16), grads[0], grads[1], grads[2], grads[3], grads[4], grads[5], grads[6], grads[7], grads[8], grads[9], grads[10], grads[11], grads[12], grads[13], grads[14], grads[15], grads[16], grads[17], grads[18])
```

```python
from functools import partial

import jax
import jax.numpy as jnp
from jax import lax
from jax.experimental import pallas as pl
from jax.experimental.pallas import tpu as pltpu
from jax.sharding import PartitionSpec as P

D = 1024
STATE = 128
AHEADS = 8
KVH = 2
HD = 64
DSSM = 1536


norm_eps = 1e-05
rope_theta = 10000.0


LOG2E = 1.4426950408889634
TILE = 256
VMEM_BYTES = 56 * 1024 * 1024


def mx(left, right, dims, precision=None):
    return lax.dot_general(
        left, right, (dims, ((), ())), preferred_element_type=jnp.float32, precision=precision
    )


NN = ((1,), (0,))
NT = ((1,), (1,))
TN = ((0,), (0,))


def lane_half(values, which):
    lane = lax.broadcasted_iota(jnp.int32, values.shape, 1)
    keep = (lane < HD) if which == 0 else (lane >= HD)
    return jnp.where(keep, values, jnp.zeros_like(values))


def swap_halves(values):
    lane = lax.broadcasted_iota(jnp.int32, values.shape, 1)
    width = values.shape[1]
    return jnp.where(
        lane % HD < HD // 2, pltpu.roll(values, width - HD // 2, 1), pltpu.roll(values, HD // 2, 1)
    )


def shift_masks(seg_col, length):
    place = lax.broadcasted_iota(jnp.int32, (length, 128), 0)
    seg = jnp.broadcast_to(seg_col, (length, 128))
    return [
        jnp.where((place >= off) & (pltpu.roll(seg, off, 0) == seg), 1.0, 0.0) for off in (1, 2, 3)
    ]


def scan_lanes(values, reverse):
    width = values.shape[1]
    lane = lax.broadcasted_iota(jnp.int32, values.shape, 1)
    step = 1
    while step < width:
        if reverse:
            values = values + jnp.where(lane < width - step, pltpu.roll(values, width - step, 1), 0.0)
        else:
            values = values + jnp.where(lane >= step, pltpu.roll(values, step, 1), 0.0)
        step *= 2
    return values


def tile_mask(seg_row, seg_col, t, s, diagonal):
    same = seg_col[pl.ds(t, TILE), :] == seg_row[:, pl.ds(s, TILE)]
    if diagonal:
        rows = lax.broadcasted_iota(jnp.int32, (TILE, TILE), 0)
        cols = lax.broadcasted_iota(jnp.int32, (TILE, TILE), 1)
        same = same & (rows >= cols)
    return same


def decays(dcol, rows, h, t, s, diagonal):
    gap = dcol[pl.ds(t, TILE), h : h + 1] - rows[8 + h : 9 + h, pl.ds(s, TILE)]
    if diagonal:
        gap = jnp.minimum(gap, rows[16 + h : 17 + h, pl.ds(s, TILE)])
    return jnp.exp2(gap)


def wide_mask(seg_row, seg_col, t, extent):
    rows = lax.broadcasted_iota(jnp.int32, (TILE, extent), 0) + t
    cols = lax.broadcasted_iota(jnp.int32, (TILE, extent), 1)
    return (seg_col[t : t + TILE, :] == seg_row[:, :extent]) & (rows >= cols)


def mixer_forward(
    heads, conv, bc, gate, query, kv, step, seg_row, seg_col, taps, per_head, skip, cos, sin,
    gated, att, pre, scan, bcr, qr, kk, lse, rows, dcol,
    xm,
):
    length, chan = conv.shape
    masks = shift_masks(seg_col[...], length)
    for i in range((chan + 256) // 128):
        lanes = slice(i * 128, (i + 1) * 128)
        if i * 128 < chan:
            signal = conv[:, lanes]
        else:
            signal = bc[:, i * 128 - chan : (i + 1) * 128 - chan].astype(jnp.float32)
        total = taps[4:5, lanes] + taps[3:4, lanes] * signal
        for off in (1, 2, 3):
            total = total + taps[3 - off : 4 - off, lanes] * (pltpu.roll(signal, off, 0) * masks[off - 1])
        pre[:, lanes] = total
        low = (total * jax.nn.sigmoid(total)).astype(jnp.bfloat16)
        if i * 128 < chan:
            xm[2 * i] = lane_half(low, 0)
            xm[2 * i + 1] = lane_half(low, 1)
        else:
            bcr[:, i * 128 - chan : (i + 1) * 128 - chan] = low
    stepped = step[...] + per_head[:, 0:1]
    size = jnp.maximum(stepped, 0.0) + jnp.log1p(jnp.exp(-jnp.abs(stepped)))
    decay = scan_lanes(size * per_head[:, 1:2], False)
    log_size = jnp.log2(size)
    rows[0:8, :] = decay
    rows[8:16, :] = decay - log_size
    rows[16:24, :] = log_size
    rows[24:32, :] = size
    dcol[...] = decay.T

    def tile(t, s, diagonal):
        both = jnp.where(
            tile_mask(seg_row, seg_col, t, s, diagonal),
            mx(bcr[pl.ds(t, TILE), 128:256], bcr[pl.ds(s, TILE), 0:128], NT),
            0.0,
        )
        for pair in range(heads // 2):
            part = None
            for h in (2 * pair, 2 * pair + 1):
                mixing = (decays(dcol, rows, h, t, s, diagonal) * both).astype(jnp.bfloat16)
                one = mx(mixing, xm[h, pl.ds(s, TILE), :], NN)
                part = one if part is None else part + one
            scan[pl.ds(t, TILE), pair * 128 : (pair + 1) * 128] += part

    scan[...] = jnp.zeros_like(scan)

    @pl.loop(0, length // TILE)
    def _(ti):
        t = pl.multiple_of(ti * TILE, TILE)

        @pl.loop(0, ti)
        def _(si):
            tile(t, pl.multiple_of(si * TILE, TILE), False)

        tile(t, t, True)

    for i in range(chan // 128):
        lanes = slice(i * 128, (i + 1) * 128)
        value = pre[:, lanes]
        whole = scan[:, lanes] + skip[:, lanes] * (value * jax.nn.sigmoid(value))
        gate_now = gate[:, lanes]
        gated[:, lanes] = whole * (gate_now * jax.nn.sigmoid(gate_now))

    query_now = query[...]
    qr[...] = (query_now * cos[...] + swap_halves(query_now) * sin[...]).astype(jnp.bfloat16)
    key_now = kv[:, 0:128].astype(jnp.float32)
    kk[...] = (key_now * cos[...] + swap_halves(key_now) * sin[...]).astype(jnp.bfloat16)
    for ti in range(length // TILE):
        t, extent = ti * TILE, (ti + 1) * TILE
        allowed = wide_mask(seg_row, seg_col, t, extent)
        out = None
        for h in range(2):
            scores = mx(lane_half(qr[t : t + TILE, :], h), kk[:extent, :], NT) * HD**-0.5
            scores = jnp.where(allowed, scores, -1000000000.0)
            top = jnp.max(scores, axis=1, keepdims=True)
            exponents = jnp.exp(scores - top)
            total = jnp.sum(exponents, axis=1, keepdims=True)
            weights = (exponents * (1.0 / total)).astype(jnp.bfloat16)
            lse[t : t + TILE, h : h + 1] = top + jnp.log(total)
            one = mx(weights, lane_half(kv[:extent, 128:256], h), NN)
            out = one if out is None else out + one
        att[t : t + TILE, :] = out.astype(jnp.bfloat16)


def mixer_backward(
    heads, d_gated, d_att, conv, bc, gate, pre, scan, bcr, qr, kk, kv, att, lse, rows, dcol, seg_row, seg_col, step,
    taps, per_head, skip, cos, sin, pick, kv_lanes,
    d_gate, d_conv, d_query, d_shared, d_step, g_taps, g_skip, g_head,
    xm, ds, dx, db, dc, dq, dk, dv,
):
    length, chan = conv.shape
    f32, bf = jnp.float32, jnp.bfloat16
    for i in range(chan // 128):
        lanes = slice(i * 128, (i + 1) * 128)
        value, gate_now, grad = pre[:, lanes], gate[:, lanes], d_gated[:, lanes]
        inner = value * jax.nn.sigmoid(value)
        sig = jax.nn.sigmoid(gate_now)
        whole = scan[:, lanes] + skip[:, lanes] * inner
        d_gate[:, lanes] = (grad * whole * sig * (1.0 + gate_now * (1.0 - sig))).astype(bf)
        d_whole = grad * gate_now * sig
        dx[:, lanes] = jnp.zeros_like(d_whole)
        g_skip[:, lanes] = jnp.sum(d_whole * inner, axis=0, keepdims=True)
        d_low = d_whole.astype(bf)
        ds[2 * i] = lane_half(d_low, 0)
        ds[2 * i + 1] = lane_half(d_low, 1)
        xm[:, lanes] = inner.astype(bf)
    db[...] = jnp.zeros_like(db)
    dc[...] = jnp.zeros_like(dc)

    def tile(t, s, diagonal):
        allowed = tile_mask(seg_row, seg_col, t, s, diagonal)
        input_b, input_c = bcr[pl.ds(s, TILE), 0:128], bcr[pl.ds(t, TILE), 128:256]
        both = jnp.where(allowed, mx(input_c, input_b, NT), 0.0)
        d_both = None
        for pair in range(heads // 2):
            part = None
            lanes = slice(pair * 128, (pair + 1) * 128)
            for h in (2 * pair, 2 * pair + 1):
                factor = decays(dcol, rows, h, t, s, diagonal)
                mixing = (factor * both).astype(bf)
                grad = ds[h, pl.ds(t, TILE), :]
                one = mx(mixing, grad, TN)
                part = one if part is None else part + one
                d_one = mx(grad, xm[pl.ds(s, TILE), lanes], NT) * factor
                d_both = d_one if d_both is None else d_both + d_one
            dx[pl.ds(s, TILE), lanes] += part
        d_both = jnp.where(allowed, d_both, 0.0).astype(bf)
        dc[pl.ds(t, TILE), :] += mx(d_both, input_b, NN)
        db[pl.ds(s, TILE), :] += mx(d_both, input_c, TN)

    @pl.loop(0, length // TILE)
    def _(ti):
        t = pl.multiple_of(ti * TILE, TILE)

        @pl.loop(0, ti)
        def _(si):
            tile(t, pl.multiple_of(si * TILE, TILE), False)

        tile(t, t, True)

    high = lax.Precision.HIGHEST
    d_sum = jnp.zeros((8, length), f32)
    by_col = jnp.zeros((8, length), f32)
    for i in range(chan // 128):
        lanes = slice(i * 128, (i + 1) * 128)
        d_low = (ds[2 * i] + ds[2 * i + 1]).astype(f32)
        by_col = by_col + mx(pick[:, lanes], xm[:, lanes].astype(f32) * dx[:, lanes], NT, high)
        d_sum = d_sum + mx(pick[:, lanes], d_low * scan[:, lanes], NT, high)
    d_sum = d_sum - by_col
    back = scan_lanes(d_sum, True) * (per_head[:, 1:2] * (1.0 / LOG2E))
    stepped = step[...] + per_head[:, 0:1]
    size = rows[24:32, :]
    sig = jax.nn.sigmoid(stepped)
    ratio = jnp.where(size > 1e-30, sig / jnp.maximum(size, 1e-30), 1.0)
    d_stepped = back * sig + by_col * ratio
    d_step[...] = d_stepped
    lane = lax.broadcasted_iota(jnp.int32, (8, 128), 1)
    g_head[...] = jnp.where(
        lane == 0,
        jnp.sum(d_stepped, axis=1, keepdims=True),
        jnp.where(lane == 1, jnp.sum(back * size, axis=1, keepdims=True), 0.0),
    )

    masks = shift_masks(seg_col[...], length)
    for i in range((chan + 256) // 128):
        lanes = slice(i * 128, (i + 1) * 128)
        value = pre[:, lanes]
        sig = jax.nn.sigmoid(value)
        if i * 128 < chan:
            signal = conv[:, lanes]
            gate_now = gate[:, lanes]
            d_value = dx[:, lanes] + skip[:, lanes] * (d_gated[:, lanes] * gate_now * jax.nn.sigmoid(gate_now))
        else:
            signal = bc[:, i * 128 - chan : (i + 1) * 128 - chan].astype(f32)
            d_value = db[...] if i * 128 == chan else dc[...]
        d_value = d_value * sig * (1.0 + value * (1.0 - sig))
        d_signal = taps[3:4, lanes] * d_value
        g_taps[4:5, lanes] = jnp.sum(d_value, axis=0, keepdims=True)
        g_taps[3:4, lanes] = jnp.sum(d_value * signal, axis=0, keepdims=True)
        for off in (1, 2, 3):
            kept = d_value * masks[off - 1]
            g_taps[3 - off : 4 - off, lanes] = jnp.sum(kept * pltpu.roll(signal, off, 0), axis=0, keepdims=True)
            d_signal = d_signal + taps[3 - off : 4 - off, lanes] * pltpu.roll(kept, length - off, 0)
        if i * 128 < chan:
            d_conv[:, lanes] = d_signal.astype(bf)
        else:
            d_shared[i - chan // 128] = d_signal
    g_taps[5:8, :] = jnp.zeros((3, chan + 256), f32)

    dk[...] = jnp.zeros_like(dk)
    dv[...] = jnp.zeros_like(dv)
    for ti in range(length // TILE):
        t, extent = ti * TILE, (ti + 1) * TILE
        allowed = wide_mask(seg_row, seg_col, t, extent)
        d_out = d_att[t : t + TILE, :]
        product = d_out * att[t : t + TILE, :].astype(f32)
        d_low = d_out.astype(bf)
        d_query_now = None
        d_key = None
        d_value = None
        for h in range(2):
            q_now, d_now = lane_half(qr[t : t + TILE, :], h), lane_half(d_low, h)
            scores = mx(q_now, kk[:extent, :], NT) * HD**-0.5
            weights = jnp.where(allowed, jnp.exp(scores - lse[t : t + TILE, h : h + 1]), 0.0)
            delta = jnp.sum(lane_half(product, h), axis=1, keepdims=True)
            d_weights = mx(d_now, kv[:extent, 128:256], NT)
            d_scores = (weights * (d_weights - delta)).astype(bf)
            one_q = mx(d_scores, lane_half(kk[:extent, :], h), NN)
            one_k = mx(d_scores, q_now, TN)
            one_v = mx(weights.astype(bf), d_now, TN)
            d_query_now = one_q if h == 0 else d_query_now + one_q
            d_key = one_k if h == 0 else d_key + one_k
            d_value = one_v if h == 0 else d_value + one_v
        dq[t : t + TILE, :] = d_query_now * HD**-0.5
        dk[:extent, :] += d_key * HD**-0.5
        dv[:extent, :] += d_value
    turned = dq[...]
    d_query[...] = (turned * cos[...] + swap_halves(turned * sin[...])).astype(bf)
    turned = dk[...]
    turned = turned * cos[...] + swap_halves(turned * sin[...])
    d_shared[2] = (turned + pltpu.roll(turned, HD, 1)) * kv_lanes[...]
    turned = dv[...]
    d_shared[3] = (turned + pltpu.roll(turned, HD, 1)) * kv_lanes[...]


def call_forward(heads, *operands):
    conv = operands[0]
    length, chan = conv.shape
    f32, bf = jnp.float32, jnp.bfloat16
    shapes = [
        ((length, chan), f32),
        ((length, 128), bf),
        ((length, chan + 256), f32),
        ((length, chan), f32),
        ((length, 256), bf),
        ((length, 128), bf),
        ((length, 128), bf),
        ((length, 2), f32),
        ((32, length), f32),
        ((length, 8), f32),
    ]
    return pl.pallas_call(
        partial(mixer_forward, heads),
        out_shape=[jax.ShapeDtypeStruct(s, d) for s, d in shapes],
        scratch_shapes=[pltpu.VMEM((heads, length, 128), bf)],
        compiler_params=pltpu.CompilerParams(vmem_limit_bytes=VMEM_BYTES),
        cost_estimate=pl.CostEstimate(flops=3 * 10**9, bytes_accessed=16 * 10**6, transcendentals=6 * 10**6),
        name="mixer_forward",
    )(*operands)


def call_backward(heads, *operands):
    length, chan = operands[2].shape
    f32, bf = jnp.float32, jnp.bfloat16
    shapes = [
        ((length, chan), bf),
        ((length, chan), bf),
        ((length, 128), bf),
        ((4, length, 128), f32),
        ((8, length), f32),
        ((8, chan + 256), f32),
        ((1, chan), f32),
        ((8, 128), f32),
    ]
    return pl.pallas_call(
        partial(mixer_backward, heads),
        out_shape=[jax.ShapeDtypeStruct(s, d) for s, d in shapes],
        scratch_shapes=[
            pltpu.VMEM((length, chan), bf),
            pltpu.VMEM((heads, length, 128), bf),
            pltpu.VMEM((length, chan), f32),
        ]
        + [pltpu.VMEM((length, 128), f32) for _ in range(5)],
        compiler_params=pltpu.CompilerParams(vmem_limit_bytes=VMEM_BYTES),
        cost_estimate=pl.CostEstimate(flops=8 * 10**9, bytes_accessed=24 * 10**6, transcendentals=8 * 10**6),
        name="mixer_backward",
    )(*operands)


BF = jnp.bfloat16
F32 = jnp.float32


def flip(values, axis, bits):
    size = lax.axis_size(axis)
    return lax.ppermute(values, axis, [(i, i ^ bits) for i in range(size)])


def swap(values):
    size = lax.axis_size("row")
    return lax.ppermute(
        values, ("row", "col"), [(i * size + j, j * size + i) for i in range(size) for j in range(size)]
    )


def gather_rows(values):
    far = flip(values, "row", 2)
    near = flip(values, "row", 1)
    return [values, near, far, flip(far, "row", 1)]


def total(values, axis):
    values = values + flip(values, axis, 1)
    return values + flip(values, axis, 2)


def scatter_sum(block):
    sent = jnp.stack([block(1).astype(BF), block(3).astype(BF)])
    got = flip(sent, "row", 1)
    passed = (block(2) + got[1].astype(F32)).astype(BF)
    return block(0) + got[0].astype(F32) + flip(passed, "row", 2).astype(F32)


def fetch(block, axis):
    size = lax.axis_size("row")
    offset = lax.axis_index("row") ^ lax.axis_index("col")
    width = block.shape[axis]
    shape = list(block.shape)
    shape[axis] = width * size
    whole = jnp.zeros(shape, block.dtype)
    for k in range(size):
        perm = [(i * size + j, j * size + (i ^ k)) for i in range(size) for j in range(size)]
        got = lax.ppermute(block, ("row", "col"), perm)
        whole = lax.dynamic_update_slice_in_dim(whole, got, (offset ^ k) * width, axis)
    return whole


def deliver(grad, axis):
    size = lax.axis_size("row")
    offset = lax.axis_index("row") ^ lax.axis_index("col")
    width = grad.shape[axis] // size
    low = grad.astype(BF)
    result = 0.0
    for k in range(size):
        perm = [(j * size + (i ^ k), i * size + j) for i in range(size) for j in range(size)]
        part = lax.dynamic_slice_in_dim(low, (offset ^ k) * width, width, axis)
        result = result + lax.ppermute(part, ("row", "col"), perm).astype(F32)
    return dp_total(result)


def after(values, done):
    return lax.optimization_barrier((values, done))[0]


def gather_share(block, axis):
    size = lax.axis_size("row")
    row = lax.axis_index("row")
    whole = lax.all_gather(block, "col", axis=0, tiled=False)
    own = [lax.dynamic_index_in_dim(whole, row ^ k, 0, False) for k in range(size)]
    return jnp.concatenate([own[0]] + [flip(own[k], "row", k) for k in range(1, size)], axis=axis)


def scatter_share(grad, axis):
    size = lax.axis_size("row")
    row = lax.axis_index("row")
    parts = jnp.split(grad.astype(BF), size, axis=axis)
    got = jnp.stack([parts[0]] + [flip(parts[k], "row", k) for k in range(1, size)])
    ordered = jnp.stack([lax.dynamic_index_in_dim(got, row ^ j, 0, False) for j in range(size)])
    return dp_total(lax.psum_scatter(ordered, "col", scatter_dimension=0, tiled=False).astype(F32))


def dp_total(values):
    size = lax.axis_size("dp")
    if size == 2:
        low = values.astype(BF)
        return low.astype(F32) + lax.ppermute(low, "dp", [(0, 1), (1, 0)]).astype(F32)
    return lax.psum(values, "dp")


def dot(left, right):
    return lax.dot_general(left, right, (((1,), (0,)), ((), ())), preferred_element_type=F32)


def dot_t(left, right):
    return lax.dot_general(left, right, (((1,), (1,)), ((), ())), preferred_element_type=F32)


def t_dot(left, right):
    return lax.dot_general(left, right, (((0,), (0,)), ((), ())), preferred_element_type=F32)


def columns(values, k):
    width = values.shape[1] // 4
    return values[:, k * width : (k + 1) * width]


def rms_scale(values):
    return lax.rsqrt(jnp.mean(values * values, axis=1, keepdims=True) + norm_eps)


def norm_back(values, scale, gain, d_normed, inner_sum, count):
    d_values = scale * (d_normed * gain[None, :]) - values * (scale * scale * scale * inner_sum / count)
    d_gain = jnp.sum(values * scale * d_normed, axis=0)
    return (d_values, d_gain)


def gate_back(gate_proj, up_proj, d_inner):
    sigmoid_gate = jax.nn.sigmoid(gate_proj)
    d_gate = d_inner * up_proj * sigmoid_gate * (1.0 + gate_proj * (1.0 - sigmoid_gate))
    d_up = d_inner * gate_proj * sigmoid_gate
    return (d_gate.astype(BF), d_up.astype(BF))


def pad_row(values, width):
    return jnp.pad(values, (0, width - values.shape[0]))[None, :]


def row_sum(values):
    return jnp.sum(values, axis=1)


def spread(vector):
    return vector.reshape(-1, 128)


def shards(
    tokens,
    segments,
    cotangent,
    norm_in,
    w_gate_ssm,
    w_conv_in,
    w_step,
    w_query,
    w_shared,
    conv_main,
    conv_side,
    step_bias,
    decay_log,
    skip_gain,
    norm_ssm,
    w_ssm_out,
    w_att_out,
    norm_mlp,
    w_gate,
    w_up,
    w_down,
):
    row = lax.axis_index("row")
    length = segments.shape[1]
    heads = step_bias.shape[0]
    chan = w_gate_ssm.shape[1]
    att = w_query.shape[1]
    side = w_shared.shape[1]
    units = w_gate.shape[1]

    x_blocks = gather_rows(tokens)
    in_share = fetch(jnp.concatenate([w_shared, w_conv_in, w_gate_ssm, w_query], axis=1), 0)
    step_share = fetch(jnp.pad(w_step.T, ((0, 16 - heads), (0, 0))), 1)
    small = swap(
        jnp.concatenate(
            [
                segments.astype(F32),
                jnp.pad(
                    jnp.concatenate(
                        [
                            conv_main,
                            norm_ssm[None, :],
                            pad_row(jnp.concatenate([step_bias, decay_log, skip_gain]), chan),
                        ],
                        axis=0,
                    ),
                    ((0, 0), (0, length - chan)),
                ),
            ],
            axis=0,
        )
    )
    segment = small[0:1].astype(jnp.int32)
    conv_main = small[1:6, :chan]
    norm_ssm = small[6, :chan]
    step_bias, decay_log, skip_gain = (small[7, i * heads : (i + 1) * heads] for i in range(3))
    gains = jnp.concatenate(gather_rows(jnp.stack([norm_in, norm_mlp])), axis=1)
    out_share = gather_share(after(jnp.concatenate([w_ssm_out, w_att_out], axis=0), in_share), 1)
    mlp_share = gather_share(after(jnp.concatenate([w_gate, w_up], axis=1), out_share), 0)
    down_share = gather_share(after(w_down, mlp_share), 1)
    d_out = jnp.concatenate(gather_rows(cotangent), axis=1)

    x_all = jnp.concatenate(x_blocks, axis=1).astype(F32)
    scale_in = rms_scale(x_all)
    hidden_in = (x_all * scale_in * gains[0][None, :]).astype(BF)
    projected = dot(hidden_in, in_share)
    shared_own = projected[:, :side]
    conv_in = projected[:, side : side + chan]
    gate_ssm = projected[:, side + chan : side + 2 * chan]
    query_in = projected[:, side + 2 * chan :]
    step_rows = dot_t(step_share, hidden_in)
    shared_rel = jnp.stack(gather_rows(shared_own.astype(BF)))
    shared_abs = [lax.dynamic_index_in_dim(shared_rel, row ^ j, 0, False) for j in range(4)]
    kv_index = row * (att // HD) // (AHEADS // KVH)
    key_own = lax.dynamic_slice_in_dim(shared_abs[2], kv_index * HD, HD, 1)
    value_own = lax.dynamic_slice_in_dim(shared_abs[3], kv_index * HD, HD, 1)
    kv = jnp.concatenate([key_own, key_own, value_own, value_own], axis=1)
    state_in = jnp.concatenate(shared_abs[:2], axis=1)

    powers = jnp.arange(HD // 2).astype(F32) * (2.0 / HD)
    angles = jnp.arange(length).astype(F32)[:, None] * (rope_theta ** (-powers))[None, :]
    cosine = jnp.tile(jnp.cos(angles), (1, 4))
    sine = jnp.sin(angles)
    sine = jnp.concatenate([-sine, sine, -sine, sine], axis=1)
    seg_row = segment
    seg_col = segment.reshape(length, 1)
    taps = jnp.pad(jnp.concatenate([conv_main, conv_side], axis=1), ((0, 3), (0, 0)))
    per_head = jnp.pad(
        jnp.stack([step_bias, -jnp.exp(decay_log) * LOG2E], axis=1), ((0, 8 - heads), (0, 126))
    )
    skip = jnp.repeat(skip_gain, chan // heads)[None, :]
    step_in = step_rows[:8]
    gated, attended, pre, scan, bcr, qr, kk, lse, rows, dcol = call_forward(
        heads, conv_in, state_in, gate_ssm, query_in, kv, step_in, seg_row, seg_col, taps, per_head, skip,
        cosine, sine,
    )

    square = total(spread(row_sum(gated * gated)), "row").reshape(-1, 1)
    scale_ssm = lax.rsqrt(square / DSSM + norm_eps)
    normed = (gated * scale_ssm * norm_ssm[None, :]).astype(BF)
    mix = jnp.concatenate([normed, attended], axis=1)
    inputs = tokens.astype(F32)
    mixed = inputs + scatter_sum(lambda k: dot(mix, columns(out_share, k)))
    mixed_all = jnp.concatenate(gather_rows(mixed.astype(BF)), axis=1).astype(F32)
    scale_mlp = rms_scale(mixed_all)
    hidden_mlp = (mixed_all * scale_mlp * gains[1][None, :]).astype(BF)
    gate_up = dot(hidden_mlp, mlp_share)
    gate_proj = gate_up[:, :units]
    up_proj = gate_up[:, units:]
    inner_mlp = (jax.nn.silu(gate_proj) * up_proj).astype(BF)
    result = mixed + scatter_sum(lambda k: dot(inner_mlp, columns(down_share, k)))

    d_inner = dot_t(d_out, down_share)
    d_gate_up = jnp.concatenate(gate_back(gate_proj, up_proj, d_inner), axis=1)
    inner_mlp_sum = total(spread(row_sum(gate_up * d_gate_up.astype(F32))), "row").reshape(-1, 1)
    rows_of = lambda share, k: share[k * D // 4 : (k + 1) * D // 4]
    d_hidden_mlp = scatter_sum(lambda k: dot_t(d_gate_up, rows_of(mlp_share, k)))
    d_mixed_norm, grad_norm_mlp = norm_back(
        mixed, scale_mlp, norm_mlp, d_hidden_mlp, inner_mlp_sum / scale_mlp, D
    )
    d_mixed = cotangent.astype(F32) + d_mixed_norm
    d_mixed_all = jnp.concatenate(gather_rows(d_mixed.astype(BF)), axis=1)
    grad_gate_up = scatter_share(t_dot(hidden_mlp, d_gate_up), 0)
    grad_down = scatter_share(t_dot(inner_mlp, d_out), 1)

    d_branch_in = dot_t(d_mixed_all, out_share)
    d_normed = d_branch_in[:, :chan]
    inner_ssm_sum = total(spread(row_sum(gated * norm_ssm[None, :] * d_normed)), "row").reshape(-1, 1)
    d_gated, grad_norm_ssm = norm_back(gated, scale_ssm, norm_ssm, d_normed, inner_ssm_sum, DSSM)
    grad_out = scatter_share(t_dot(mix, d_mixed_all), 1)
    lane = jnp.arange(chan)[None, :] // (chan // heads)
    pick = (lane == jnp.arange(8)[:, None]).astype(F32)
    kv_lanes = (jnp.arange(128)[None, :] // HD == kv_index).astype(F32)
    d_gate, d_conv, d_query, d_whole, d_step, g_taps, g_skip, g_head = call_backward(
        heads, d_gated, d_branch_in[:, chan:], conv_in, state_in, gate_ssm, pre, scan, bcr, qr, kk, kv, attended,
        lse, rows, dcol, seg_row, seg_col, step_in, taps, per_head, skip, cosine, sine, pick, kv_lanes,
    )
    g_skip = jnp.sum(g_skip.reshape(heads, -1), axis=1)
    d_shared = scatter_sum(lambda k: lax.dynamic_index_in_dim(d_whole, row ^ k, 0, False))
    d_projected = jnp.concatenate([d_shared.astype(BF), d_conv, d_gate, d_query], axis=1)
    d_step = jnp.pad(d_step, ((0, 8), (0, 0))).astype(BF)
    inner_in_sum = (
        row_sum(projected * d_projected.astype(F32)) + jnp.sum(step_rows * d_step.astype(F32), axis=0)
    )
    inner_in_sum = total(spread(inner_in_sum), "row").reshape(-1, 1)
    d_hidden_in = scatter_sum(
        lambda k: dot_t(d_projected, rows_of(in_share, k)) + t_dot(d_step, columns(step_share, k))
    )
    grad_in = deliver(t_dot(hidden_in, d_projected), 0)
    grad_step = deliver(dot(d_step, hidden_in), 1)
    d_inputs, grad_norm_in = norm_back(inputs, scale_in, norm_in, d_hidden_in, inner_in_sum / scale_in, D)
    d_tokens = d_mixed + d_inputs

    wide = max(chan, conv_side.shape[1])
    by_head = jnp.concatenate(
        [
            g_taps[:5, :chan],
            grad_norm_ssm[None, :],
            pad_row(jnp.concatenate([g_head[:heads, 0], g_head[:heads, 1], g_skip]), chan),
        ],
        axis=0,
    )
    fields = [jnp.pad(by_head, ((0, 0), (0, wide - chan)))]
    fields.append(jnp.pad(g_taps[:5, chan:], ((0, 0), (0, wide - conv_side.shape[1]))))
    fields.append(pad_row(grad_norm_mlp, wide))
    fields.append(pad_row(grad_norm_in, wide))
    sums = jnp.concatenate(fields, axis=0)
    sums = total(sums, "col")
    size = lax.axis_size("dp")
    if size == 2:
        sums = sums + lax.ppermute(sums, "dp", [(0, 1), (1, 0)])
    else:
        sums = lax.psum(sums, "dp")
    by_head = swap(sums[:7])
    grad_side = total(sums[7:12], "row")
    return (
        result.astype(BF),
        d_tokens,
        sums[13, : norm_in.shape[0]],
        grad_in[:, side + chan : side + 2 * chan],
        grad_in[:, side : side + chan],
        grad_step[:heads].T,
        grad_in[:, side + 2 * chan :],
        grad_in[:, :side],
        by_head[:5, :chan],
        grad_side[:, : conv_side.shape[1]],
        by_head[6, :heads],
        by_head[6, heads : 2 * heads],
        by_head[6, 2 * heads : 3 * heads],
        by_head[5, :chan],
        grad_out[:chan],
        grad_out[chan:],
        sums[12, : norm_mlp.shape[0]],
        grad_gate_up[:, :units],
        grad_gate_up[:, units:],
        grad_down,
    )


def solution(mesh):
    return jax.shard_map(
        shards,
        mesh=mesh,
        in_specs=(
            P(("dp", "col"), "row"),
            P(("dp", "row"), None),
            P(("dp", "col"), "row"),
            P("row"),
            P("row", "col"),
            P("row", "col"),
            P("row", "col"),
            P("row", "col"),
            P("row", "col"),
            P(None, "col"),
            P(),
            P("col"),
            P("col"),
            P("col"),
            P("col"),
            P("col", "row"),
            P("col", "row"),
            P("row"),
            P("row", "col"),
            P("row", "col"),
            P("col", "row"),
        ),
        out_specs=(
            P(("dp", "col"), "row"),
            P(("dp", "col"), "row"),
            P("row"),
            P("row", "col"),
            P("row", "col"),
            P("row", "col"),
            P("row", "col"),
            P("row", "col"),
            P(None, "col"),
            P(),
            P("col"),
            P("col"),
            P("col"),
            P("col"),
            P("col", "row"),
            P("col", "row"),
            P("row"),
            P("row", "col"),
            P("row", "col"),
            P("col", "row"),
        ),
        check_vma=False,
    )
```

```python
from functools import partial

import jax
import jax.numpy as jnp
from jax import lax
from jax.experimental import pallas as pl
from jax.experimental.pallas import tpu as pltpu
from jax.sharding import PartitionSpec as P

D = 1024
STATE = 128
AHEADS = 8
KVH = 2
HD = 64
DSSM = 1536


norm_eps = 1e-05
rope_theta = 10000.0


LOG2E = 1.4426950408889634
TILE = 256
VMEM_BYTES = 56 * 1024 * 1024


def mx(left, right, dims, precision=None):
    return lax.dot_general(
        left, right, (dims, ((), ())), preferred_element_type=jnp.float32, precision=precision
    )


NN = ((1,), (0,))
NT = ((1,), (1,))
TN = ((0,), (0,))


def lane_half(values, which):
    lane = lax.broadcasted_iota(jnp.int32, values.shape, 1)
    keep = (lane < HD) if which == 0 else (lane >= HD)
    return jnp.where(keep, values, jnp.zeros_like(values))


def swap_halves(values):
    lane = lax.broadcasted_iota(jnp.int32, values.shape, 1)
    width = values.shape[1]
    return jnp.where(
        lane % HD < HD // 2, pltpu.roll(values, width - HD // 2, 1), pltpu.roll(values, HD // 2, 1)
    )


def shift_masks(seg_col, length):
    place = lax.broadcasted_iota(jnp.int32, (length, 128), 0)
    seg = jnp.broadcast_to(seg_col, (length, 128))
    return [
        jnp.where((place >= off) & (pltpu.roll(seg, off, 0) == seg), 1.0, 0.0) for off in (1, 2, 3)
    ]


def scan_lanes(values, reverse):
    width = values.shape[1]
    lane = lax.broadcasted_iota(jnp.int32, values.shape, 1)
    step = 1
    while step < width:
        if reverse:
            values = values + jnp.where(lane < width - step, pltpu.roll(values, width - step, 1), 0.0)
        else:
            values = values + jnp.where(lane >= step, pltpu.roll(values, step, 1), 0.0)
        step *= 2
    return values


def tile_mask(seg_row, seg_col, t, s, diagonal):
    same = seg_col[pl.ds(t, TILE), :] == seg_row[:, pl.ds(s, TILE)]
    if diagonal:
        rows = lax.broadcasted_iota(jnp.int32, (TILE, TILE), 0)
        cols = lax.broadcasted_iota(jnp.int32, (TILE, TILE), 1)
        same = same & (rows >= cols)
    return same


def decays(dcol, rows, h, t, s, diagonal):
    gap = dcol[pl.ds(t, TILE), h : h + 1] - rows[8 + h : 9 + h, pl.ds(s, TILE)]
    if diagonal:
        gap = jnp.minimum(gap, rows[16 + h : 17 + h, pl.ds(s, TILE)])
    return jnp.exp2(gap)


def wide_mask(seg_row, seg_col, t, extent):
    rows = lax.broadcasted_iota(jnp.int32, (TILE, extent), 0) + t
    cols = lax.broadcasted_iota(jnp.int32, (TILE, extent), 1)
    return (seg_col[t : t + TILE, :] == seg_row[:, :extent]) & (rows >= cols)


def mixer_forward(
    heads, conv, bc, gate, query, kv, step, seg_row, seg_col, taps, per_head, skip, cos, sin,
    gated, att, pre, scan, bcr, qr, kk, lse, rows, dcol, square,
    xm,
):
    length, chan = conv.shape
    masks = shift_masks(seg_col[...], length)
    for i in range((chan + 256) // 128):
        lanes = slice(i * 128, (i + 1) * 128)
        if i * 128 < chan:
            signal = conv[:, lanes]
        else:
            signal = bc[:, i * 128 - chan : (i + 1) * 128 - chan].astype(jnp.float32)
        total = taps[4:5, lanes] + taps[3:4, lanes] * signal
        for off in (1, 2, 3):
            total = total + taps[3 - off : 4 - off, lanes] * (pltpu.roll(signal, off, 0) * masks[off - 1])
        pre[:, lanes] = total
        low = (total * jax.nn.sigmoid(total)).astype(jnp.bfloat16)
        if i * 128 < chan:
            xm[2 * i] = lane_half(low, 0)
            xm[2 * i + 1] = lane_half(low, 1)
        else:
            bcr[:, i * 128 - chan : (i + 1) * 128 - chan] = low
    stepped = step[...] + per_head[:, 0:1]
    size = jnp.maximum(stepped, 0.0) + jnp.log1p(jnp.exp(-jnp.abs(stepped)))
    decay = scan_lanes(size * per_head[:, 1:2], False)
    log_size = jnp.log2(size)
    rows[0:8, :] = decay
    rows[8:16, :] = decay - log_size
    rows[16:24, :] = log_size
    rows[24:32, :] = size
    dcol[...] = decay.T

    def tile(t, s, diagonal):
        both = jnp.where(
            tile_mask(seg_row, seg_col, t, s, diagonal),
            mx(bcr[pl.ds(t, TILE), 128:256], bcr[pl.ds(s, TILE), 0:128], NT),
            0.0,
        )
        for pair in range(heads // 2):
            part = None
            for h in (2 * pair, 2 * pair + 1):
                mixing = (decays(dcol, rows, h, t, s, diagonal) * both).astype(jnp.bfloat16)
                one = mx(mixing, xm[h, pl.ds(s, TILE), :], NN)
                part = one if part is None else part + one
            scan[pl.ds(t, TILE), pair * 128 : (pair + 1) * 128] += part

    scan[...] = jnp.zeros_like(scan)

    @pl.loop(0, length // TILE)
    def _(ti):
        t = pl.multiple_of(ti * TILE, TILE)

        @pl.loop(0, ti)
        def _(si):
            tile(t, pl.multiple_of(si * TILE, TILE), False)

        tile(t, t, True)

    squares = []
    for i in range(chan // 128):
        lanes = slice(i * 128, (i + 1) * 128)
        value = pre[:, lanes]
        whole = scan[:, lanes] + skip[:, lanes] * (value * jax.nn.sigmoid(value))
        gate_now = gate[:, lanes]
        whole = whole * (gate_now * jax.nn.sigmoid(gate_now))
        gated[:, lanes] = whole
        squares.append(whole * whole)
    square[...] = row_totals(*squares)

    query_now = query[...]
    qr[...] = (query_now * cos[...] + swap_halves(query_now) * sin[...]).astype(jnp.bfloat16)
    key_now = kv[:, 0:128].astype(jnp.float32)
    kk[...] = (key_now * cos[...] + swap_halves(key_now) * sin[...]).astype(jnp.bfloat16)
    for ti in range(length // TILE):
        t, extent = ti * TILE, (ti + 1) * TILE
        allowed = wide_mask(seg_row, seg_col, t, extent)
        out = None
        for h in range(2):
            scores = mx(lane_half(qr[t : t + TILE, :], h), kk[:extent, :], NT) * HD**-0.5
            scores = jnp.where(allowed, scores, -1000000000.0)
            top = jnp.max(scores, axis=1, keepdims=True)
            exponents = jnp.exp(scores - top)
            total = jnp.sum(exponents, axis=1, keepdims=True)
            weights = (exponents * (1.0 / total)).astype(jnp.bfloat16)
            lse[t : t + TILE, h : h + 1] = top + jnp.log(total)
            one = mx(weights, lane_half(kv[:extent, 128:256], h), NN)
            out = one if out is None else out + one
        att[t : t + TILE, :] = out.astype(jnp.bfloat16)


def mixer_backward(
    heads, d_normed, gated, scale_ssm, cross, gain, d_att, conv, bc, gate, pre, scan, bcr, qr, kk, kv, att, lse, rows, dcol, seg_row, seg_col, step,
    taps, per_head, skip, cos, sin, pick, kv_lanes,
    d_gate, d_conv, d_query, d_shared, d_step, g_taps, g_skip, g_head, g_norm,
    d_gated, xm, ds, dx, db, dc, dq, dk, dv,
):
    length, chan = conv.shape
    f32, bf = jnp.float32, jnp.bfloat16
    size = scale_ssm[...]
    both_scale = size * size * size * (as_column(cross[...]) * (1.0 / DSSM))
    for i in range(chan // 128):
        lanes = slice(i * 128, (i + 1) * 128)
        value, gate_now = pre[:, lanes], gate[:, lanes]
        scaled, mixed_now = d_normed[:, lanes] * scale_ssm[...], gated[:, lanes]
        grad = scaled * gain[:, lanes] - mixed_now * both_scale
        d_gated[:, lanes] = grad
        g_norm[:, lanes] = jnp.sum(mixed_now * scaled, axis=0, keepdims=True)
        inner = value * jax.nn.sigmoid(value)
        sig = jax.nn.sigmoid(gate_now)
        whole = scan[:, lanes] + skip[:, lanes] * inner
        d_gate[:, lanes] = (grad * whole * sig * (1.0 + gate_now * (1.0 - sig))).astype(bf)
        d_whole = grad * gate_now * sig
        dx[:, lanes] = jnp.zeros_like(d_whole)
        g_skip[:, lanes] = jnp.sum(d_whole * inner, axis=0, keepdims=True)
        d_low = d_whole.astype(bf)
        ds[2 * i] = lane_half(d_low, 0)
        ds[2 * i + 1] = lane_half(d_low, 1)
        xm[:, lanes] = inner.astype(bf)
    db[...] = jnp.zeros_like(db)
    dc[...] = jnp.zeros_like(dc)

    def tile(t, s, diagonal):
        allowed = tile_mask(seg_row, seg_col, t, s, diagonal)
        input_b, input_c = bcr[pl.ds(s, TILE), 0:128], bcr[pl.ds(t, TILE), 128:256]
        both = jnp.where(allowed, mx(input_c, input_b, NT), 0.0)
        d_both = None
        for pair in range(heads // 2):
            part = None
            lanes = slice(pair * 128, (pair + 1) * 128)
            for h in (2 * pair, 2 * pair + 1):
                factor = decays(dcol, rows, h, t, s, diagonal)
                mixing = (factor * both).astype(bf)
                grad = ds[h, pl.ds(t, TILE), :]
                one = mx(mixing, grad, TN)
                part = one if part is None else part + one
                d_one = mx(grad, xm[pl.ds(s, TILE), lanes], NT) * factor
                d_both = d_one if d_both is None else d_both + d_one
            dx[pl.ds(s, TILE), lanes] += part
        d_both = jnp.where(allowed, d_both, 0.0).astype(bf)
        dc[pl.ds(t, TILE), :] += mx(d_both, input_b, NN)
        db[pl.ds(s, TILE), :] += mx(d_both, input_c, TN)

    @pl.loop(0, length // TILE)
    def _(ti):
        t = pl.multiple_of(ti * TILE, TILE)

        @pl.loop(0, ti)
        def _(si):
            tile(t, pl.multiple_of(si * TILE, TILE), False)

        tile(t, t, True)

    high = lax.Precision.HIGHEST
    d_sum = jnp.zeros((8, length), f32)
    by_col = jnp.zeros((8, length), f32)
    for i in range(chan // 128):
        lanes = slice(i * 128, (i + 1) * 128)
        d_low = (ds[2 * i] + ds[2 * i + 1]).astype(f32)
        by_col = by_col + mx(pick[:, lanes], xm[:, lanes].astype(f32) * dx[:, lanes], NT, high)
        d_sum = d_sum + mx(pick[:, lanes], d_low * scan[:, lanes], NT, high)
    d_sum = d_sum - by_col
    back = scan_lanes(d_sum, True) * (per_head[:, 1:2] * (1.0 / LOG2E))
    stepped = step[...] + per_head[:, 0:1]
    size = rows[24:32, :]
    sig = jax.nn.sigmoid(stepped)
    ratio = jnp.where(size > 1e-30, sig / jnp.maximum(size, 1e-30), 1.0)
    d_stepped = back * sig + by_col * ratio
    d_step[...] = d_stepped
    lane = lax.broadcasted_iota(jnp.int32, (8, 128), 1)
    g_head[...] = jnp.where(
        lane == 0,
        jnp.sum(d_stepped, axis=1, keepdims=True),
        jnp.where(lane == 1, jnp.sum(back * size, axis=1, keepdims=True), 0.0),
    )

    masks = shift_masks(seg_col[...], length)
    for i in range((chan + 256) // 128):
        lanes = slice(i * 128, (i + 1) * 128)
        value = pre[:, lanes]
        sig = jax.nn.sigmoid(value)
        if i * 128 < chan:
            signal = conv[:, lanes]
            gate_now = gate[:, lanes]
            d_value = dx[:, lanes] + skip[:, lanes] * (d_gated[:, lanes] * gate_now * jax.nn.sigmoid(gate_now))
        else:
            signal = bc[:, i * 128 - chan : (i + 1) * 128 - chan].astype(f32)
            d_value = db[...] if i * 128 == chan else dc[...]
        d_value = d_value * sig * (1.0 + value * (1.0 - sig))
        d_signal = taps[3:4, lanes] * d_value
        g_taps[4:5, lanes] = jnp.sum(d_value, axis=0, keepdims=True)
        g_taps[3:4, lanes] = jnp.sum(d_value * signal, axis=0, keepdims=True)
        for off in (1, 2, 3):
            kept = d_value * masks[off - 1]
            g_taps[3 - off : 4 - off, lanes] = jnp.sum(kept * pltpu.roll(signal, off, 0), axis=0, keepdims=True)
            d_signal = d_signal + taps[3 - off : 4 - off, lanes] * pltpu.roll(kept, length - off, 0)
        if i * 128 < chan:
            d_conv[:, lanes] = d_signal.astype(bf)
        else:
            d_shared[i - chan // 128] = d_signal
    g_taps[5:8, :] = jnp.zeros((3, chan + 256), f32)

    dk[...] = jnp.zeros_like(dk)
    dv[...] = jnp.zeros_like(dv)
    for ti in range(length // TILE):
        t, extent = ti * TILE, (ti + 1) * TILE
        allowed = wide_mask(seg_row, seg_col, t, extent)
        d_out = d_att[t : t + TILE, :]
        product = d_out * att[t : t + TILE, :].astype(f32)
        d_low = d_out.astype(bf)
        d_query_now = None
        d_key = None
        d_value = None
        for h in range(2):
            q_now, d_now = lane_half(qr[t : t + TILE, :], h), lane_half(d_low, h)
            scores = mx(q_now, kk[:extent, :], NT) * HD**-0.5
            weights = jnp.where(allowed, jnp.exp(scores - lse[t : t + TILE, h : h + 1]), 0.0)
            delta = jnp.sum(lane_half(product, h), axis=1, keepdims=True)
            d_weights = mx(d_now, kv[:extent, 128:256], NT)
            d_scores = (weights * (d_weights - delta)).astype(bf)
            one_q = mx(d_scores, lane_half(kk[:extent, :], h), NN)
            one_k = mx(d_scores, q_now, TN)
            one_v = mx(weights.astype(bf), d_now, TN)
            d_query_now = one_q if h == 0 else d_query_now + one_q
            d_key = one_k if h == 0 else d_key + one_k
            d_value = one_v if h == 0 else d_value + one_v
        dq[t : t + TILE, :] = d_query_now * HD**-0.5
        dk[:extent, :] += d_key * HD**-0.5
        dv[:extent, :] += d_value
    turned = dq[...]
    d_query[...] = (turned * cos[...] + swap_halves(turned * sin[...])).astype(bf)
    turned = dk[...]
    turned = turned * cos[...] + swap_halves(turned * sin[...])
    d_shared[2] = (turned + pltpu.roll(turned, HD, 1)) * kv_lanes[...]
    turned = dv[...]
    d_shared[3] = (turned + pltpu.roll(turned, HD, 1)) * kv_lanes[...]


def without_held(body, used, held, *refs):
    body(*refs[:used], *refs[used + held :])


def rows_spec(width):
    return pl.BlockSpec((TILE, width), lambda i: (i, 0))


def row_spec():
    return pl.BlockSpec((1, TILE), lambda i: (0, i))


def whole_spec(shape):
    return pl.BlockSpec(shape, lambda i: (0,) * len(shape))


def pair_spec():
    return pl.BlockSpec((2, TILE, 256), lambda i: (0, i, 0))


def smem_spec():
    return pl.BlockSpec(memory_space=pltpu.SMEM)


def token_call(body, name, length, ins, outs, scratch, flops, held=()):
    ins = ins + [(a, pl.BlockSpec(memory_space=pl.ANY)) for a in held]
    count = len(ins)

    def without_held(*refs):
        body(*refs[: count - len(held)], *refs[count:])

    size = sum(int(a.size) * a.dtype.itemsize for a, _ in ins)
    return pl.pallas_call(
        without_held,
        grid=(length // TILE,),
        in_specs=[s for _, s in ins],
        out_specs=[s for _, _, s in outs],
        out_shape=[jax.ShapeDtypeStruct(s, d) for s, d, _ in outs],
        scratch_shapes=scratch,
        compiler_params=pltpu.CompilerParams(vmem_limit_bytes=VMEM_BYTES),
        cost_estimate=pl.CostEstimate(flops=flops, bytes_accessed=size, transcendentals=0),
        name=name,
    )(*[a for a, _ in ins])


def row_totals(*values):
    pieces = [value[:, i : i + 128] for value in values for i in range(0, value.shape[1], 128)]
    return mx(jnp.ones((8, 128), jnp.float32), sum(pieces[1:], pieces[0]), NT, lax.Precision.HIGHEST)[0:1]


def as_column(row):
    return jnp.broadcast_to(row, (8, row.shape[1])).T[:, 0:1]


def stack_halves(share, mine, other, place, by_rows):
    bit = place[0]
    for j, (one, two) in enumerate(zip(mine, other)):
        half, width = one.shape
        k = place[1] ^ j
        for ref, side in ((one, bit), (two, 1 - bit)):
            if by_rows:
                first = pl.multiple_of(k * (2 * half) + side * half, half)
                share[pl.ds(first, half), :] = ref[...]
            else:
                first = pl.multiple_of(side * half, half)
                share[pl.ds(first, half), pl.ds(pl.multiple_of(k * width, width), width)] = ref[...]


def project(x0, x1, x2, x3, g0, g1, g2, g3, a0, a1, a2, a3, b0, b1, b2, b3, place, share, gains, hidden, scale, shared, conv, gate, query, step):
    chan = conv.shape[1]

    @pl.when(pl.program_id(0) == 0)
    def _():
        stack_halves(share, (a0, a1, a2, a3), (b0, b1, b2, b3), place, True)
        for k, g in enumerate((g0, g1, g2, g3)):
            parts = g[...].astype(jnp.float32)
            lanes = slice(k * 256, (k + 1) * 256)
            gains[0:1, lanes] = parts[0:1] + parts[1:2] + parts[2:3]
            gains[1:2, lanes] = parts[3:4] + parts[4:5] + parts[5:6]

    values = jnp.concatenate([x[...] for x in (x0, x1, x2, x3)], axis=1).astype(jnp.float32)
    size = lax.rsqrt(jnp.mean(values * values, axis=1, keepdims=True) + norm_eps)
    low = (values * size * gains[0:1, :]).astype(jnp.bfloat16)
    hidden[...] = low
    scale[...] = size
    out = mx(low, share[...], NN)
    shared[...] = out[:, :128].astype(jnp.bfloat16)
    conv[...] = out[:, 128 : 128 + chan]
    step[...] = out[:, 128 + chan : 256 + chan].T[:8]
    gate[...] = out[:, 256 + chan : 256 + 2 * chan]
    query[...] = out[:, 256 + 2 * chan :]


def put_blocks(value, sent, kept):
    sent[0] = value[:, 256:512].astype(jnp.bfloat16)
    sent[1] = value[:, 768:1024].astype(jnp.bfloat16)
    kept[0] = value[:, 0:256]
    kept[1] = value[:, 512:768]


def out_project(gated, att, square, gain, a0, a1, a2, a3, b0, b1, b2, b3, place, share, mix, scale, sent, kept):
    chan = gated.shape[1]

    @pl.when(pl.program_id(0) == 0)
    def _():
        stack_halves(share, (a0, a1, a2, a3), (b0, b1, b2, b3), place, False)

    size = lax.rsqrt(as_column(square[...]) / DSSM + norm_eps)
    scale[...] = size
    low = jnp.concatenate([(gated[...] * size * gain[...]).astype(jnp.bfloat16), att[...]], axis=1)
    mix[...] = low
    put_blocks(mx(low, share[...], NN), sent, kept)


def feed_forward(
    m0, m1, m2, m3, gains, e0, e1, e2, e3, f0, f1, f2, f3, a0, a1, a2, a3, b0, b1, b2, b3, c0, c1, c2, c3, place,
    hidden, inner, d_gate_up, scale, cross, sent, kept, sent_down, kept_down, d_out,
    share, down,
):
    units = inner.shape[1]
    bf = jnp.bfloat16

    @pl.when(pl.program_id(0) == 0)
    def _():
        stack_halves(share, (e0, e1, e2, e3), (f0, f1, f2, f3), place, True)
        stack_halves(down, (a0, a1, a2, a3), (b0, b1, b2, b3), place, False)

    values = jnp.concatenate([m[...] for m in (m0, m1, m2, m3)], axis=1).astype(jnp.float32)
    size = lax.rsqrt(jnp.mean(values * values, axis=1, keepdims=True) + norm_eps)
    low = (values * size * gains[1:2, :]).astype(bf)
    hidden[...] = low
    scale[...] = size
    out = mx(low, share[...], NN)
    gate, up = out[:, :units], out[:, units:]
    grad = jnp.concatenate([c[...] for c in (c0, c1, c2, c3)], axis=1)
    d_out[...] = grad
    d_inner = mx(grad, down[...], NT)
    sig = jax.nn.sigmoid(gate)
    both = gate * sig
    unit = (both * up).astype(bf)
    inner[...] = unit
    d_gate = (d_inner * up * (sig + both * (1.0 - sig))).astype(bf)
    d_up = (d_inner * both).astype(bf)
    cross[...] = row_totals(gate * d_gate.astype(jnp.float32) + up * d_up.astype(jnp.float32))
    d_low = jnp.concatenate([d_gate, d_up], axis=1)
    d_gate_up[...] = d_low
    put_blocks(mx(d_low, share[...], NT), sent, kept)
    put_blocks(mx(unit, down[...], NN), sent_down, kept_down)


def out_backward(d0, d1, d2, d3, share, gated, gain, d_normed, d_att, cross, d_mixed):
    chan = gated.shape[1]
    grad = jnp.concatenate([d[...] for d in (d0, d1, d2, d3)], axis=1)
    d_mixed[...] = grad
    out = mx(grad, share[...], NT)
    d_normed[...] = out[:, :chan]
    d_att[...] = out[:, chan:]
    cross[...] = row_totals(gated[...] * gain[...] * out[:, :chan])


def in_backward(d_shared, d_conv, d_gate, d_query, d_step, shared, conv, gate, query, step, share, d_late, cross, sent, kept):
    bf, f32 = jnp.bfloat16, jnp.float32
    steps = jnp.concatenate([d_step[...], jnp.zeros((120, TILE), f32)], axis=0).T
    low = jnp.concatenate([d_shared[...].astype(bf), d_conv[...], steps.astype(bf), d_gate[...], d_query[...]], axis=1)
    d_late[...] = jnp.concatenate([d_shared[...].astype(bf), steps.astype(bf)], axis=1)
    pairs = ((shared, d_shared), (conv, d_conv), (gate, d_gate), (query, d_query))
    products = [a[...].astype(f32) * b[...].astype(f32) for a, b in pairs]
    cross[...] = row_totals(*products) + jnp.sum(step[...] * d_step[...], axis=0, keepdims=True)
    put_blocks(mx(low, share[...], NT), sent, kept)


def call_forward(heads, held, *operands):
    conv = operands[0]
    length, chan = conv.shape
    f32, bf = jnp.float32, jnp.bfloat16
    shapes = [
        ((length, chan), f32),
        ((length, 128), bf),
        ((length, chan + 256), f32),
        ((length, chan), f32),
        ((length, 256), bf),
        ((length, 128), bf),
        ((length, 128), bf),
        ((length, 2), f32),
        ((32, length), f32),
        ((length, 8), f32),
        ((1, length), f32),
    ]
    return pl.pallas_call(
        partial(without_held, partial(mixer_forward, heads), len(operands), len(held)),
        out_shape=[jax.ShapeDtypeStruct(s, d) for s, d in shapes],
        scratch_shapes=[pltpu.VMEM((heads, length, 128), bf)],
        in_specs=[pl.BlockSpec(memory_space=pltpu.VMEM)] * len(operands)
        + [pl.BlockSpec(memory_space=pl.ANY)] * len(held),
        compiler_params=pltpu.CompilerParams(vmem_limit_bytes=VMEM_BYTES),
        cost_estimate=pl.CostEstimate(flops=3 * 10**9, bytes_accessed=16 * 10**6, transcendentals=6 * 10**6),
        name="mixer_forward",
    )(*operands, *held)


def call_backward(heads, held, *operands):
    length, chan = operands[1].shape
    f32, bf = jnp.float32, jnp.bfloat16
    shapes = [
        ((length, chan), bf),
        ((length, chan), bf),
        ((length, 128), bf),
        ((4, length, 128), f32),
        ((8, length), f32),
        ((8, chan + 256), f32),
        ((1, chan), f32),
        ((8, 128), f32),
        ((1, chan), f32),
    ]
    return pl.pallas_call(
        partial(without_held, partial(mixer_backward, heads), len(operands), len(held)),
        out_shape=[jax.ShapeDtypeStruct(s, d) for s, d in shapes],
        scratch_shapes=[
            pltpu.VMEM((length, chan), f32),
            pltpu.VMEM((length, chan), bf),
            pltpu.VMEM((heads, length, 128), bf),
            pltpu.VMEM((length, chan), f32),
        ]
        + [pltpu.VMEM((length, 128), f32) for _ in range(5)],
        in_specs=[pl.BlockSpec(memory_space=pltpu.VMEM)] * len(operands)
        + [pl.BlockSpec(memory_space=pl.ANY)] * len(held),
        compiler_params=pltpu.CompilerParams(vmem_limit_bytes=VMEM_BYTES),
        cost_estimate=pl.CostEstimate(flops=8 * 10**9, bytes_accessed=24 * 10**6, transcendentals=8 * 10**6),
        name="mixer_backward",
    )(*operands, *held)


BF = jnp.bfloat16
F32 = jnp.float32


def flip(values, axis, bits):
    size = lax.axis_size(axis)
    return lax.ppermute(values, axis, [(i, i ^ bits) for i in range(size)])


def swap(values):
    size = lax.axis_size("row")
    return lax.ppermute(
        values, ("row", "col"), [(i * size + j, j * size + i) for i in range(size) for j in range(size)]
    )


def gather_rows(values):
    far = flip(values, "row", 2)
    near = flip(values, "row", 1)
    return [values, near, far, flip(far, "row", 1)]


def total(values, axis):
    values = values + flip(values, axis, 1)
    return values + flip(values, axis, 2)


def scatter_sum(sent, kept):
    got = flip(sent, "row", 1)
    passed = (kept[1] + got[1].astype(F32)).astype(BF)
    return kept[0] + got[0].astype(F32) + flip(passed, "row", 2).astype(F32)


def tie(values, *done):
    def body(*refs):
        pass

    anywhere = pl.BlockSpec(memory_space=pl.ANY)
    return pl.pallas_call(
        body,
        out_shape=jax.ShapeDtypeStruct(values.shape, values.dtype),
        in_specs=[anywhere] * (1 + len(done)),
        out_specs=anywhere,
        input_output_aliases={0: 0},
        name="tie",
    )(values, *done)


def partner(values):
    size = lax.axis_size("dp")
    return lax.ppermute(values, "dp", [(i, i ^ 1) for i in range(size)])


def own_half(block):
    half = block.shape[0] // 2
    return lax.dynamic_slice_in_dim(block, (lax.axis_index("dp") & 1) * half, half, 0)


def fetch_halves(half):
    size = lax.axis_size("row")
    got = []
    for k in range(size):
        perm = [(i * size + j, j * size + (i ^ k)) for i in range(size) for j in range(size)]
        got.append(lax.ppermute(half, ("row", "col"), perm))
    return got, [partner(one) for one in got]


def gather_halves(half):
    got = lax.all_gather(half, "col", axis=0, tiled=False)
    row = lax.axis_index("row")
    own = [lax.dynamic_index_in_dim(got, row ^ k, 0, False) for k in range(4)]
    mine = [own[0]] + [flip(own[k], "row", k) for k in (1, 2, 3)]
    return mine, [partner(one) for one in mine], got


def split_share(grad, axis):
    size = lax.axis_size("row")
    row = lax.axis_index("row")
    parts = jnp.stack(jnp.split(grad.astype(BF), size, axis=axis))
    return jnp.stack([lax.dynamic_index_in_dim(parts, row ^ j, 0, False) for j in range(size)])


def halve(blocks, done=None):
    if lax.axis_size("dp") != 2:
        return blocks
    half = blocks.shape[1] // 2
    bit = lax.axis_index("dp") & 1
    kept = lax.dynamic_slice_in_dim(blocks, bit * half, half, 1)
    sent = lax.dynamic_slice_in_dim(blocks, (1 - bit) * half, half, 1)
    if done is not None:
        kept = tie(kept, done)
    return (kept.astype(F32) + partner(sent).astype(F32)).astype(BF)


def join(half):
    if lax.axis_size("dp") != 2:
        return dp_total(half.astype(F32))
    half = half.astype(BF)
    other = partner(half)
    first = (lax.axis_index("dp") & 1) == 0
    return jnp.concatenate([jnp.where(first, half, other), jnp.where(first, other, half)], axis=0).astype(F32)


def sum_cols(blocks):
    return lax.psum_scatter(blocks, "col", scatter_dimension=0, tiled=False)


def sum_flips(blocks):
    col = lax.axis_index("col")
    result = lax.dynamic_index_in_dim(blocks, col, 0, False).astype(F32)
    for k in (1, 2, 3):
        result = result + flip(lax.dynamic_index_in_dim(blocks, col ^ k, 0, False), "col", k).astype(F32)
    return result.astype(BF)


def dp_sum(values):
    size = lax.axis_size("dp")
    return values + partner(values) if size == 2 else lax.psum(values, "dp")


def dp_total(values):
    size = lax.axis_size("dp")
    if size == 2:
        low = values.astype(BF)
        return low.astype(F32) + lax.ppermute(low, "dp", [(0, 1), (1, 0)]).astype(F32)
    return lax.psum(values, "dp")


def t_dot(left, right):
    return lax.dot_general(left, right, (((0,), (0,)), ((), ())), preferred_element_type=F32)


def norm_back(values, scale, gain, d_normed, inner_sum, count):
    d_values = scale * (d_normed * gain[None, :]) - values * (scale * scale * scale * inner_sum / count)
    d_gain = jnp.sum(values * scale * d_normed, axis=0)
    return (d_values, d_gain)


def pad_row(values, width):
    return jnp.pad(values, (0, width - values.shape[0]))[None, :]


def shards(
    tokens,
    segments,
    cotangent,
    norm_in,
    w_gate_ssm,
    w_conv_in,
    w_step,
    w_query,
    w_shared,
    conv_main,
    conv_side,
    step_bias,
    decay_log,
    skip_gain,
    norm_ssm,
    w_ssm_out,
    w_att_out,
    norm_mlp,
    w_gate,
    w_up,
    w_down,
):
    row = lax.axis_index("row")
    length = segments.shape[1]
    heads = step_bias.shape[0]
    chan = w_gate_ssm.shape[1]
    att = w_query.shape[1]
    side = w_shared.shape[1]
    units = w_gate.shape[1]

    parts = []
    for gain in (norm_in, norm_mlp):
        for _ in range(3):
            part = lax.reduce_precision(gain, 8, 7)
            parts.append(part.astype(BF))
            gain = gain - part
    payload = jnp.concatenate([tokens, jnp.pad(jnp.stack(parts), ((0, 10), (0, 0)))], axis=0)
    x_blocks = gather_rows(payload)
    small = swap(
        jnp.concatenate(
            [
                segments.astype(F32),
                jnp.pad(
                    jnp.concatenate(
                        [
                            conv_main,
                            norm_ssm[None, :],
                            pad_row(jnp.concatenate([step_bias, decay_log, skip_gain]), chan),
                        ],
                        axis=0,
                    ),
                    ((0, 0), (0, length - chan)),
                ),
            ],
            axis=0,
        )
    )
    segment = small[0:1].astype(jnp.int32)
    conv_main = small[1:6, :chan]
    gain_ssm = small[6:7, :chan]
    step_bias, decay_log, skip_gain = (small[7, i * heads : (i + 1) * heads] for i in range(3))
    in_block = jnp.concatenate(
        [w_shared, w_conv_in, jnp.pad(w_step, ((0, 0), (0, 128 - heads))), w_gate_ssm, w_query], axis=1
    )
    in_mine, in_other = fetch_halves(own_half(in_block))
    pair_half = jnp.concatenate([own_half(jnp.concatenate([w_ssm_out, w_att_out], axis=0)), own_half(w_down)], axis=0)
    mlp_half = own_half(jnp.concatenate([w_gate, w_up], axis=1))
    pair_mine, pair_other, _ = gather_halves(tie(pair_half, *in_mine[:4]))
    mlp_mine, mlp_other, mlp_got = gather_halves(tie(mlp_half, *in_mine[:4]))
    cot_blocks = gather_rows(cotangent)
    bit = lax.axis_index("dp") & 1
    place = jnp.stack([bit, jnp.zeros_like(bit)]).astype(jnp.int32)
    place_in = jnp.stack([bit, row ^ lax.axis_index("col")]).astype(jnp.int32)

    bf, f32 = BF, F32
    weights = [(w, whole_spec(w.shape)) for w in in_mine + in_other]
    wide = 256 + 2 * chan + att
    gain_spec = pl.BlockSpec((16, 256), lambda i: (length // 16, 0))
    in_share, gains, hidden_in, scale_in, shared_own, conv_in, gate_ssm, query_in, step_in = token_call(
        project, "project", length,
        [(x, rows_spec(256)) for x in x_blocks] + [(x, gain_spec) for x in x_blocks] + weights + [(place_in, smem_spec())],
        [
            ((D, wide), bf, whole_spec((D, wide))),
            ((2, D), f32, whole_spec((2, D))),
            ((length, D), bf, rows_spec(D)),
            ((length, 1), f32, rows_spec(1)),
            ((length, side), bf, rows_spec(side)),
            ((length, chan), f32, rows_spec(chan)),
            ((length, chan), f32, rows_spec(chan)),
            ((length, att), f32, rows_spec(att)),
            ((8, length), f32, pl.BlockSpec((8, TILE), lambda i: (0, i))),
        ],
        [], 2 * length * D * wide
    )
    shared_rel = jnp.stack(gather_rows(shared_own))
    shared_abs = [lax.dynamic_index_in_dim(shared_rel, row ^ j, 0, False) for j in range(4)]
    kv_index = row * (att // HD) // (AHEADS // KVH)
    key_own = lax.dynamic_slice_in_dim(shared_abs[2], kv_index * HD, HD, 1)
    value_own = lax.dynamic_slice_in_dim(shared_abs[3], kv_index * HD, HD, 1)
    kv = jnp.concatenate([key_own, key_own, value_own, value_own], axis=1)
    state_in = jnp.concatenate(shared_abs[:2], axis=1)

    powers = jnp.arange(HD // 2).astype(F32) * (2.0 / HD)
    angles = jnp.arange(length).astype(F32)[:, None] * (rope_theta ** (-powers))[None, :]
    cosine = jnp.tile(jnp.cos(angles), (1, 4))
    sine = jnp.sin(angles)
    sine = jnp.concatenate([-sine, sine, -sine, sine], axis=1)
    seg_row = segment
    seg_col = segment.reshape(length, 1)
    taps = jnp.pad(jnp.concatenate([conv_main, conv_side], axis=1), ((0, 3), (0, 0)))
    per_head = jnp.pad(
        jnp.stack([step_bias, -jnp.exp(decay_log) * LOG2E], axis=1), ((0, 8 - heads), (0, 126))
    )
    skip = jnp.repeat(skip_gain, chan // heads)[None, :]
    gated, attended, pre, scan, bcr, qr, kk, lse, rows, dcol, square = call_forward(
        heads, [cot_blocks[3], mlp_got], conv_in, state_in, gate_ssm, query_in, kv, step_in, seg_row, seg_col, taps, per_head, skip,
        cosine, sine,
    )

    square = total(square, "row")
    half_out, half_down = (chan + att) // 2, units // 2
    out_spec = pl.BlockSpec((half_out, 256), lambda i: (0, 0))
    down_spec = pl.BlockSpec((half_down, 256), lambda i: (half_out // half_down, 0))
    weights = [(w, out_spec) for w in pair_mine + pair_other]
    deep = chan + att
    pair_out = [
        ((2, length, 256), bf, pair_spec()),
        ((2, length, 256), f32, pair_spec()),
    ]
    out_share, mix, scale_ssm, sent, kept = token_call(
        out_project, "out_project", length,
        [(gated, rows_spec(chan)), (attended, rows_spec(att)), (square, row_spec()), (gain_ssm, whole_spec((1, chan)))]
        + weights + [(place, smem_spec())],
        [
            ((deep, D), bf, whole_spec((deep, D))),
            ((length, deep), bf, rows_spec(deep)),
            ((length, 1), f32, rows_spec(1)),
        ] + pair_out,
        [], 2 * length * D * deep,
    )
    inputs = tokens.astype(F32)
    mixed = inputs + scatter_sum(sent, kept)
    mixed_blocks = gather_rows(tie(mixed.astype(BF), *mlp_other))

    weights = [(w, whole_spec(w.shape)) for w in mlp_mine + mlp_other]
    weights += [(w, down_spec) for w in pair_mine + pair_other]
    hidden_mlp, inner_mlp, d_gate_up, scale_mlp, cross, sent, kept, sent_down, kept_down, d_out = token_call(
        feed_forward, "feed_forward", length,
        [(m, rows_spec(256)) for m in mixed_blocks] + [(gains, whole_spec((2, D)))] + weights
        + [(c, rows_spec(256)) for c in cot_blocks] + [(place, smem_spec())],
        [
            ((length, D), bf, rows_spec(D)),
            ((length, units), bf, rows_spec(units)),
            ((length, 2 * units), bf, rows_spec(2 * units)),
            ((length, 1), f32, rows_spec(1)),
            ((1, length), f32, row_spec()),
        ] + pair_out + pair_out + [((length, D), bf, rows_spec(D))],
        [pltpu.VMEM((D, 2 * units), bf), pltpu.VMEM((units, D), bf)], 6 * length * D * 2 * units,
    )
    cross = total(cross, "row").reshape(-1, 1)
    d_hidden_mlp = scatter_sum(sent, kept)
    d_mixed_norm, grad_norm_mlp = norm_back(mixed, scale_mlp, norm_mlp, d_hidden_mlp, cross / scale_mlp, D)
    d_mixed = cotangent.astype(F32) + d_mixed_norm
    d_mixed_blocks = gather_rows(d_mixed.astype(BF))
    mlp_halves = halve(split_share(t_dot(hidden_mlp, d_gate_up), 0))
    down_halves = halve(split_share(t_dot(inner_mlp, d_out), 1))
    got_down = flip(tie(sent_down, d_mixed_blocks[3]), "row", 1)
    passed_down = (kept_down[1] + got_down[1].astype(F32)).astype(BF)
    result = mixed + kept_down[0] + got_down[0].astype(F32) + flip(passed_down, "row", 2).astype(F32)

    mlp_sum = sum_cols(mlp_halves)
    d_normed, d_att, cross, d_mixed_all = token_call(
        out_backward, "out_backward", length,
        [(d, rows_spec(256)) for d in d_mixed_blocks]
        + [(out_share, whole_spec((deep, D))), (gated, rows_spec(chan)), (gain_ssm, whole_spec((1, chan)))],
        [
            ((length, chan), f32, rows_spec(chan)),
            ((length, att), f32, rows_spec(att)),
            ((1, length), f32, row_spec()),
            ((length, D), bf, rows_spec(D)),
        ],
        [], 2 * length * D * deep, [mlp_halves, down_halves],
    )
    cross = total(cross, "row")
    out_blocks = split_share(t_dot(mix, d_mixed_all), 1)
    lane = jnp.arange(chan)[None, :] // (chan // heads)
    pick = (lane == jnp.arange(8)[:, None]).astype(F32)
    kv_lanes = (jnp.arange(128)[None, :] // HD == kv_index).astype(F32)
    d_gate, d_conv, d_query, d_whole, d_step, g_taps, g_skip, g_head, g_norm = call_backward(
        heads, [passed_down], d_normed, gated, scale_ssm, cross, gain_ssm, d_att, conv_in, state_in, gate_ssm, pre, scan, bcr, qr, kk,
        kv, attended, lse, rows, dcol, seg_row, seg_col, step_in, taps, per_head, skip, cosine, sine, pick, kv_lanes,
    )
    g_skip = jnp.sum(g_skip.reshape(heads, -1), axis=1)
    pair_sum = sum_cols(jnp.concatenate([down_halves, halve(out_blocks, d_step)], axis=1))
    early = jnp.concatenate([d_conv, d_gate, d_query], axis=1)
    early_blocks = split_share(t_dot(hidden_in, early), 0)
    to = [lax.dynamic_index_in_dim(d_whole, row ^ k, 0, False) for k in range(4)]
    d_shared = scatter_sum(jnp.stack([to[1].astype(BF), to[3].astype(BF)]), (to[0], to[2]))
    d_late, cross, sent, kept = token_call(
        in_backward, "in_backward", length,
        [
            (d_shared, rows_spec(side)), (d_conv, rows_spec(chan)), (d_gate, rows_spec(chan)), (d_query, rows_spec(att)),
            (d_step, pl.BlockSpec((8, TILE), lambda i: (0, i))),
            (shared_own, rows_spec(side)), (conv_in, rows_spec(chan)), (gate_ssm, rows_spec(chan)),
            (query_in, rows_spec(att)), (step_in, pl.BlockSpec((8, TILE), lambda i: (0, i))),
            (in_share, whole_spec((D, wide))),
        ],
        [((length, side + 128), bf, rows_spec(side + 128)), ((1, length), f32, row_spec())] + pair_out,
        [], 2 * length * D * wide, [mlp_sum],
    )
    cross = total(cross, "row")
    got = flip(sent, "row", 1)
    passed = (kept[1] + got[1].astype(F32)).astype(BF)
    d_hidden_in = kept[0] + got[0].astype(F32) + flip(passed, "row", 2).astype(F32)
    late_halves = halve(split_share(t_dot(hidden_in, tie(d_late, passed)), 0))
    early_halves = halve(early_blocks, d_hidden_in)
    in_sum = sum_flips(jnp.concatenate([early_halves, late_halves], axis=2))
    grad_in = join(swap(in_sum))
    grad_early, grad_late = grad_in[:, : 2 * chan + att], grad_in[:, 2 * chan + att :]
    grad_gate_up = join(swap(tie(mlp_sum, d_hidden_in)))
    pair_far = swap(tie(pair_sum, d_hidden_in))
    grad_down, grad_out = join(pair_far[: pair_far.shape[0] * units // (units + deep)]), join(pair_far[pair_far.shape[0] * units // (units + deep) :])
    d_inputs, grad_norm_in = norm_back(inputs, scale_in, norm_in, d_hidden_in, cross.reshape(-1, 1) / scale_in, D)
    d_tokens = d_mixed + d_inputs

    room = max(chan, conv_side.shape[1])
    by_head = jnp.concatenate(
        [
            g_taps[:5, :chan],
            g_norm,
            pad_row(jnp.concatenate([g_head[:heads, 0], g_head[:heads, 1], g_skip]), chan),
        ],
        axis=0,
    )
    fields = [jnp.pad(by_head, ((0, 0), (0, room - chan)))]
    fields.append(jnp.pad(g_taps[:5, chan:], ((0, 0), (0, room - conv_side.shape[1]))))
    fields.append(pad_row(grad_norm_mlp, room))
    fields.append(pad_row(grad_norm_in, room))
    sums = dp_sum(total(jnp.concatenate(fields, axis=0), "col"))
    by_head = swap(sums[:7])
    grad_side = total(sums[7:12], "row")
    return (
        result.astype(BF),
        d_tokens,
        sums[13, : norm_in.shape[0]],
        grad_early[:, chan : 2 * chan],
        grad_early[:, :chan],
        grad_late[:, side : side + heads],
        grad_early[:, 2 * chan :],
        grad_late[:, :side],
        by_head[:5, :chan],
        grad_side[:, : conv_side.shape[1]],
        by_head[6, :heads],
        by_head[6, heads : 2 * heads],
        by_head[6, 2 * heads : 3 * heads],
        by_head[5, :chan],
        grad_out[:chan],
        grad_out[chan:],
        sums[12, : norm_mlp.shape[0]],
        grad_gate_up[:, :units],
        grad_gate_up[:, units:],
        grad_down,
    )


def solution(mesh):
    return jax.shard_map(
        shards,
        mesh=mesh,
        in_specs=(
            P(("dp", "col"), "row"),
            P(("dp", "row"), None),
            P(("dp", "col"), "row"),
            P("row"),
            P("row", "col"),
            P("row", "col"),
            P("row", "col"),
            P("row", "col"),
            P("row", "col"),
            P(None, "col"),
            P(),
            P("col"),
            P("col"),
            P("col"),
            P("col"),
            P("col", "row"),
            P("col", "row"),
            P("row"),
            P("row", "col"),
            P("row", "col"),
            P("col", "row"),
        ),
        out_specs=(
            P(("dp", "col"), "row"),
            P(("dp", "col"), "row"),
            P("row"),
            P("row", "col"),
            P("row", "col"),
            P("row", "col"),
            P("row", "col"),
            P("row", "col"),
            P(None, "col"),
            P(),
            P("col"),
            P("col"),
            P("col"),
            P("col"),
            P("col", "row"),
            P("col", "row"),
            P("row"),
            P("row", "col"),
            P("row", "col"),
            P("col", "row"),
        ),
        check_vma=False,
    )
```

```python
from functools import partial

import jax
import jax.numpy as jnp
from jax import lax
from jax.experimental import pallas as pl
from jax.experimental.pallas import tpu as pltpu
from jax.sharding import PartitionSpec as P

D = 1024
STATE = 128
AHEADS = 8
KVH = 2
HD = 64
DSSM = 1536


norm_eps = 1e-05
rope_theta = 10000.0


LOG2E = 1.4426950408889634
TILE = 256
VMEM_BYTES = 56 * 1024 * 1024


def mx(left, right, dims, precision=None):
    return lax.dot_general(
        left, right, (dims, ((), ())), preferred_element_type=jnp.float32, precision=precision
    )


NN = ((1,), (0,))
NT = ((1,), (1,))
TN = ((0,), (0,))


def lane_half(values, which):
    lane = lax.broadcasted_iota(jnp.int32, values.shape, 1)
    keep = (lane < HD) if which == 0 else (lane >= HD)
    return jnp.where(keep, values, jnp.zeros_like(values))


def swap_halves(values):
    lane = lax.broadcasted_iota(jnp.int32, values.shape, 1)
    width = values.shape[1]
    return jnp.where(
        lane % HD < HD // 2, pltpu.roll(values, width - HD // 2, 1), pltpu.roll(values, HD // 2, 1)
    )


def shift_masks(seg_col, length):
    place = lax.broadcasted_iota(jnp.int32, (length, 128), 0)
    seg = jnp.broadcast_to(seg_col, (length, 128))
    return [
        jnp.where((place >= off) & (pltpu.roll(seg, off, 0) == seg), 1.0, 0.0) for off in (1, 2, 3)
    ]


def scan_lanes(values, reverse):
    width = values.shape[1]
    lane = lax.broadcasted_iota(jnp.int32, values.shape, 1)
    step = 1
    while step < width:
        if reverse:
            values = values + jnp.where(lane < width - step, pltpu.roll(values, width - step, 1), 0.0)
        else:
            values = values + jnp.where(lane >= step, pltpu.roll(values, step, 1), 0.0)
        step *= 2
    return values


def tile_mask(seg_row, seg_col, t, s, diagonal):
    same = seg_col[pl.ds(t, TILE), :] == seg_row[:, pl.ds(s, TILE)]
    if diagonal:
        rows = lax.broadcasted_iota(jnp.int32, (TILE, TILE), 0)
        cols = lax.broadcasted_iota(jnp.int32, (TILE, TILE), 1)
        same = same & (rows >= cols)
    return same


def decays(dcol, rows, h, t, s, diagonal):
    gap = dcol[pl.ds(t, TILE), h : h + 1] - rows[8 + h : 9 + h, pl.ds(s, TILE)]
    if diagonal:
        gap = jnp.minimum(gap, rows[16 + h : 17 + h, pl.ds(s, TILE)])
    return jnp.exp2(gap)


def wide_mask(seg_row, seg_col, t, extent):
    rows = lax.broadcasted_iota(jnp.int32, (TILE, extent), 0) + t
    cols = lax.broadcasted_iota(jnp.int32, (TILE, extent), 1)
    return (seg_col[t : t + TILE, :] == seg_row[:, :extent]) & (rows >= cols)


def mixer_forward(
    heads, conv, bc, gate, query, kv, step, seg_row, seg_col, taps, per_head, skip, cos, sin,
    gated, att, pre, scan, bcr, qr, kk, lse, rows, dcol, square,
    xm,
):
    length, chan = conv.shape
    masks = shift_masks(seg_col[...], length)
    for i in range((chan + 256) // 128):
        lanes = slice(i * 128, (i + 1) * 128)
        if i * 128 < chan:
            signal = conv[:, lanes]
        else:
            signal = bc[:, i * 128 - chan : (i + 1) * 128 - chan].astype(jnp.float32)
        total = taps[4:5, lanes] + taps[3:4, lanes] * signal
        for off in (1, 2, 3):
            total = total + taps[3 - off : 4 - off, lanes] * (pltpu.roll(signal, off, 0) * masks[off - 1])
        pre[:, lanes] = total
        low = (total * jax.nn.sigmoid(total)).astype(jnp.bfloat16)
        if i * 128 < chan:
            xm[2 * i] = lane_half(low, 0)
            xm[2 * i + 1] = lane_half(low, 1)
        else:
            bcr[:, i * 128 - chan : (i + 1) * 128 - chan] = low
    stepped = step[...] + per_head[:, 0:1]
    size = jnp.maximum(stepped, 0.0) + jnp.log1p(jnp.exp(-jnp.abs(stepped)))
    decay = scan_lanes(size * per_head[:, 1:2], False)
    log_size = jnp.log2(size)
    rows[0:8, :] = decay
    rows[8:16, :] = decay - log_size
    rows[16:24, :] = log_size
    rows[24:32, :] = size
    dcol[...] = decay.T

    def tile(t, s, diagonal):
        both = jnp.where(
            tile_mask(seg_row, seg_col, t, s, diagonal),
            mx(bcr[pl.ds(t, TILE), 128:256], bcr[pl.ds(s, TILE), 0:128], NT),
            0.0,
        )
        for pair in range(heads // 2):
            part = None
            for h in (2 * pair, 2 * pair + 1):
                mixing = (decays(dcol, rows, h, t, s, diagonal) * both).astype(jnp.bfloat16)
                one = mx(mixing, xm[h, pl.ds(s, TILE), :], NN)
                part = one if part is None else part + one
            scan[pl.ds(t, TILE), pair * 128 : (pair + 1) * 128] += part

    scan[...] = jnp.zeros_like(scan)

    @pl.loop(0, length // TILE)
    def _(ti):
        t = pl.multiple_of(ti * TILE, TILE)

        @pl.loop(0, ti)
        def _(si):
            tile(t, pl.multiple_of(si * TILE, TILE), False)

        tile(t, t, True)

    squares = []
    for i in range(chan // 128):
        lanes = slice(i * 128, (i + 1) * 128)
        value = pre[:, lanes]
        whole = scan[:, lanes] + skip[:, lanes] * (value * jax.nn.sigmoid(value))
        gate_now = gate[:, lanes]
        whole = whole * (gate_now * jax.nn.sigmoid(gate_now))
        gated[:, lanes] = whole
        squares.append(whole * whole)
    square[...] = row_totals(*squares)

    query_now = query[...]
    qr[...] = (query_now * cos[...] + swap_halves(query_now) * sin[...]).astype(jnp.bfloat16)
    key_now = kv[:, 0:128].astype(jnp.float32)
    kk[...] = (key_now * cos[...] + swap_halves(key_now) * sin[...]).astype(jnp.bfloat16)
    for ti in range(length // TILE):
        t, extent = ti * TILE, (ti + 1) * TILE
        allowed = wide_mask(seg_row, seg_col, t, extent)
        out = None
        for h in range(2):
            scores = mx(lane_half(qr[t : t + TILE, :], h), kk[:extent, :], NT) * HD**-0.5
            scores = jnp.where(allowed, scores, -1000000000.0)
            top = jnp.max(scores, axis=1, keepdims=True)
            exponents = jnp.exp(scores - top)
            total = jnp.sum(exponents, axis=1, keepdims=True)
            weights = (exponents * (1.0 / total)).astype(jnp.bfloat16)
            lse[t : t + TILE, h : h + 1] = top + jnp.log(total)
            one = mx(weights, lane_half(kv[:extent, 128:256], h), NN)
            out = one if out is None else out + one
        att[t : t + TILE, :] = out.astype(jnp.bfloat16)


def mixer_backward(
    heads, d_normed, gated, scale_ssm, cross, gain, d_att, conv, bc, gate, pre, scan, bcr, qr, kk, kv, att, lse, rows, dcol, seg_row, seg_col, step,
    taps, per_head, skip, cos, sin, pick, kv_lanes,
    d_gate, d_conv, d_query, d_shared, d_step, g_taps, g_skip, g_head, g_norm,
    d_gated, xm, ds, dx, db, dc, dq, dk, dv,
):
    length, chan = conv.shape
    f32, bf = jnp.float32, jnp.bfloat16
    size = scale_ssm[...]
    both_scale = size * size * size * (as_column(cross[...]) * (1.0 / DSSM))
    for i in range(chan // 128):
        lanes = slice(i * 128, (i + 1) * 128)
        value, gate_now = pre[:, lanes], gate[:, lanes]
        scaled, mixed_now = d_normed[:, lanes] * scale_ssm[...], gated[:, lanes]
        grad = scaled * gain[:, lanes] - mixed_now * both_scale
        d_gated[:, lanes] = grad
        g_norm[:, lanes] = jnp.sum(mixed_now * scaled, axis=0, keepdims=True)
        inner = value * jax.nn.sigmoid(value)
        sig = jax.nn.sigmoid(gate_now)
        whole = scan[:, lanes] + skip[:, lanes] * inner
        d_gate[:, lanes] = (grad * whole * sig * (1.0 + gate_now * (1.0 - sig))).astype(bf)
        d_whole = grad * gate_now * sig
        dx[:, lanes] = jnp.zeros_like(d_whole)
        g_skip[:, lanes] = jnp.sum(d_whole * inner, axis=0, keepdims=True)
        d_low = d_whole.astype(bf)
        ds[2 * i] = lane_half(d_low, 0)
        ds[2 * i + 1] = lane_half(d_low, 1)
        xm[:, lanes] = inner.astype(bf)
    db[...] = jnp.zeros_like(db)
    dc[...] = jnp.zeros_like(dc)

    def tile(t, s, diagonal):
        allowed = tile_mask(seg_row, seg_col, t, s, diagonal)
        input_b, input_c = bcr[pl.ds(s, TILE), 0:128], bcr[pl.ds(t, TILE), 128:256]
        both = jnp.where(allowed, mx(input_c, input_b, NT), 0.0)
        d_both = None
        for pair in range(heads // 2):
            part = None
            lanes = slice(pair * 128, (pair + 1) * 128)
            for h in (2 * pair, 2 * pair + 1):
                factor = decays(dcol, rows, h, t, s, diagonal)
                mixing = (factor * both).astype(bf)
                grad = ds[h, pl.ds(t, TILE), :]
                one = mx(mixing, grad, TN)
                part = one if part is None else part + one
                d_one = mx(grad, xm[pl.ds(s, TILE), lanes], NT) * factor
                d_both = d_one if d_both is None else d_both + d_one
            dx[pl.ds(s, TILE), lanes] += part
        d_both = jnp.where(allowed, d_both, 0.0).astype(bf)
        dc[pl.ds(t, TILE), :] += mx(d_both, input_b, NN)
        db[pl.ds(s, TILE), :] += mx(d_both, input_c, TN)

    @pl.loop(0, length // TILE)
    def _(ti):
        t = pl.multiple_of(ti * TILE, TILE)

        @pl.loop(0, ti)
        def _(si):
            tile(t, pl.multiple_of(si * TILE, TILE), False)

        tile(t, t, True)

    high = lax.Precision.HIGHEST
    d_sum = jnp.zeros((8, length), f32)
    by_col = jnp.zeros((8, length), f32)
    for i in range(chan // 128):
        lanes = slice(i * 128, (i + 1) * 128)
        d_low = (ds[2 * i] + ds[2 * i + 1]).astype(f32)
        by_col = by_col + mx(pick[:, lanes], xm[:, lanes].astype(f32) * dx[:, lanes], NT, high)
        d_sum = d_sum + mx(pick[:, lanes], d_low * scan[:, lanes], NT, high)
    d_sum = d_sum - by_col
    back = scan_lanes(d_sum, True) * (per_head[:, 1:2] * (1.0 / LOG2E))
    stepped = step[...] + per_head[:, 0:1]
    size = rows[24:32, :]
    sig = jax.nn.sigmoid(stepped)
    ratio = jnp.where(size > 1e-30, sig / jnp.maximum(size, 1e-30), 1.0)
    d_stepped = back * sig + by_col * ratio
    d_step[...] = d_stepped
    lane = lax.broadcasted_iota(jnp.int32, (8, 128), 1)
    g_head[...] = jnp.where(
        lane == 0,
        jnp.sum(d_stepped, axis=1, keepdims=True),
        jnp.where(lane == 1, jnp.sum(back * size, axis=1, keepdims=True), 0.0),
    )

    masks = shift_masks(seg_col[...], length)
    for i in range((chan + 256) // 128):
        lanes = slice(i * 128, (i + 1) * 128)
        value = pre[:, lanes]
        sig = jax.nn.sigmoid(value)
        if i * 128 < chan:
            signal = conv[:, lanes]
            gate_now = gate[:, lanes]
            d_value = dx[:, lanes] + skip[:, lanes] * (d_gated[:, lanes] * gate_now * jax.nn.sigmoid(gate_now))
        else:
            signal = bc[:, i * 128 - chan : (i + 1) * 128 - chan].astype(f32)
            d_value = db[...] if i * 128 == chan else dc[...]
        d_value = d_value * sig * (1.0 + value * (1.0 - sig))
        d_signal = taps[3:4, lanes] * d_value
        g_taps[4:5, lanes] = jnp.sum(d_value, axis=0, keepdims=True)
        g_taps[3:4, lanes] = jnp.sum(d_value * signal, axis=0, keepdims=True)
        for off in (1, 2, 3):
            kept = d_value * masks[off - 1]
            g_taps[3 - off : 4 - off, lanes] = jnp.sum(kept * pltpu.roll(signal, off, 0), axis=0, keepdims=True)
            d_signal = d_signal + taps[3 - off : 4 - off, lanes] * pltpu.roll(kept, length - off, 0)
        if i * 128 < chan:
            d_conv[:, lanes] = d_signal.astype(bf)
        else:
            d_shared[i - chan // 128] = d_signal
    g_taps[5:8, :] = jnp.zeros((3, chan + 256), f32)

    dk[...] = jnp.zeros_like(dk)
    dv[...] = jnp.zeros_like(dv)
    for ti in range(length // TILE):
        t, extent = ti * TILE, (ti + 1) * TILE
        allowed = wide_mask(seg_row, seg_col, t, extent)
        d_out = d_att[t : t + TILE, :]
        product = d_out * att[t : t + TILE, :].astype(f32)
        d_low = d_out.astype(bf)
        d_query_now = None
        d_key = None
        d_value = None
        for h in range(2):
            q_now, d_now = lane_half(qr[t : t + TILE, :], h), lane_half(d_low, h)
            scores = mx(q_now, kk[:extent, :], NT) * HD**-0.5
            weights = jnp.where(allowed, jnp.exp(scores - lse[t : t + TILE, h : h + 1]), 0.0)
            delta = jnp.sum(lane_half(product, h), axis=1, keepdims=True)
            d_weights = mx(d_now, kv[:extent, 128:256], NT)
            d_scores = (weights * (d_weights - delta)).astype(bf)
            one_q = mx(d_scores, lane_half(kk[:extent, :], h), NN)
            one_k = mx(d_scores, q_now, TN)
            one_v = mx(weights.astype(bf), d_now, TN)
            d_query_now = one_q if h == 0 else d_query_now + one_q
            d_key = one_k if h == 0 else d_key + one_k
            d_value = one_v if h == 0 else d_value + one_v
        dq[t : t + TILE, :] = d_query_now * HD**-0.5
        dk[:extent, :] += d_key * HD**-0.5
        dv[:extent, :] += d_value
    turned = dq[...]
    d_query[...] = (turned * cos[...] + swap_halves(turned * sin[...])).astype(bf)
    turned = dk[...]
    turned = turned * cos[...] + swap_halves(turned * sin[...])
    d_shared[2] = (turned + pltpu.roll(turned, HD, 1)) * kv_lanes[...]
    turned = dv[...]
    d_shared[3] = (turned + pltpu.roll(turned, HD, 1)) * kv_lanes[...]


def without_held(body, used, held, *refs):
    body(*refs[:used], *refs[used + held :])


def rows_spec(width):
    return pl.BlockSpec((TILE, width), lambda i: (i, 0))


def row_spec():
    return pl.BlockSpec((1, TILE), lambda i: (0, i))


def whole_spec(shape):
    return pl.BlockSpec(shape, lambda i: (0,) * len(shape))


def pair_spec():
    return pl.BlockSpec((2, TILE, 256), lambda i: (0, i, 0))


def smem_spec():
    return pl.BlockSpec(memory_space=pltpu.SMEM)


def token_call(body, name, length, ins, outs, scratch, flops, held=()):
    ins = ins + [(a, pl.BlockSpec(memory_space=pl.ANY)) for a in held]
    count = len(ins)

    def without_held(*refs):
        body(*refs[: count - len(held)], *refs[count:])

    size = sum(int(a.size) * a.dtype.itemsize for a, _ in ins)
    return pl.pallas_call(
        without_held,
        grid=(length // TILE,),
        in_specs=[s for _, s in ins],
        out_specs=[s for _, _, s in outs],
        out_shape=[jax.ShapeDtypeStruct(s, d) for s, d, _ in outs],
        scratch_shapes=scratch,
        compiler_params=pltpu.CompilerParams(vmem_limit_bytes=VMEM_BYTES),
        cost_estimate=pl.CostEstimate(flops=flops, bytes_accessed=size, transcendentals=0),
        name=name,
    )(*[a for a, _ in ins])


def row_totals(*values):
    pieces = [value[:, i : i + 128] for value in values for i in range(0, value.shape[1], 128)]
    return mx(jnp.ones((8, 128), jnp.float32), sum(pieces[1:], pieces[0]), NT, lax.Precision.HIGHEST)[0:1]


def as_column(row):
    return jnp.broadcast_to(row, (8, row.shape[1])).T[:, 0:1]


def stack_halves(share, mine, other, place, by_rows):
    bit = place[0]
    for j, (one, two) in enumerate(zip(mine, other)):
        half, width = one.shape
        k = place[1] ^ j
        for ref, side in ((one, bit), (two, 1 - bit)):
            if by_rows:
                first = pl.multiple_of(k * (2 * half) + side * half, half)
                share[pl.ds(first, half), :] = ref[...]
            else:
                first = pl.multiple_of(side * half, half)
                share[pl.ds(first, half), pl.ds(pl.multiple_of(k * width, width), width)] = ref[...]


def project(x0, x1, x2, x3, g0, g1, g2, g3, a0, a1, a2, a3, b0, b1, b2, b3, place, share, gains, hidden, scale, shared, conv, gate, query, step):
    chan = conv.shape[1]

    @pl.when(pl.program_id(0) == 0)
    def _():
        stack_halves(share, (a0, a1, a2, a3), (b0, b1, b2, b3), place, True)
        for k, g in enumerate((g0, g1, g2, g3)):
            parts = g[...].astype(jnp.float32)
            lanes = slice(k * 256, (k + 1) * 256)
            gains[0:1, lanes] = parts[0:1] + parts[1:2] + parts[2:3]
            gains[1:2, lanes] = parts[3:4] + parts[4:5] + parts[5:6]

    values = jnp.concatenate([x[...] for x in (x0, x1, x2, x3)], axis=1).astype(jnp.float32)
    size = lax.rsqrt(jnp.mean(values * values, axis=1, keepdims=True) + norm_eps)
    low = (values * size * gains[0:1, :]).astype(jnp.bfloat16)
    hidden[...] = low
    scale[...] = size
    out = mx(low, share[...], NN)
    shared[...] = out[:, :128].astype(jnp.bfloat16)
    conv[...] = out[:, 128 : 128 + chan]
    step[...] = out[:, 128 + chan : 256 + chan].T[:8]
    gate[...] = out[:, 256 + chan : 256 + 2 * chan]
    query[...] = out[:, 256 + 2 * chan :]


def put_blocks(value, sent, kept):
    sent[0] = value[:, 256:512].astype(jnp.bfloat16)
    sent[1] = value[:, 768:1024].astype(jnp.bfloat16)
    kept[0] = value[:, 0:256]
    kept[1] = value[:, 512:768]


def out_project(gated, att, square, gain, a0, a1, a2, a3, b0, b1, b2, b3, place, share, mix, scale, sent, kept):
    chan = gated.shape[1]

    @pl.when(pl.program_id(0) == 0)
    def _():
        stack_halves(share, (a0, a1, a2, a3), (b0, b1, b2, b3), place, False)

    size = lax.rsqrt(as_column(square[...]) / DSSM + norm_eps)
    scale[...] = size
    low = jnp.concatenate([(gated[...] * size * gain[...]).astype(jnp.bfloat16), att[...]], axis=1)
    mix[...] = low
    put_blocks(mx(low, share[...], NN), sent, kept)


def feed_forward(
    m0, m1, m2, m3, gains, e0, e1, e2, e3, f0, f1, f2, f3, a0, a1, a2, a3, b0, b1, b2, b3, c0, c1, c2, c3, place,
    hidden, inner, d_gate_up, scale, cross, sent, kept, sent_down, kept_down, d_out,
    share, down,
):
    units = inner.shape[1]
    bf = jnp.bfloat16

    @pl.when(pl.program_id(0) == 0)
    def _():
        stack_halves(share, (e0, e1, e2, e3), (f0, f1, f2, f3), place, True)
        stack_halves(down, (a0, a1, a2, a3), (b0, b1, b2, b3), place, False)

    values = jnp.concatenate([m[...] for m in (m0, m1, m2, m3)], axis=1).astype(jnp.float32)
    size = lax.rsqrt(jnp.mean(values * values, axis=1, keepdims=True) + norm_eps)
    low = (values * size * gains[1:2, :]).astype(bf)
    hidden[...] = low
    scale[...] = size
    out = mx(low, share[...], NN)
    gate, up = out[:, :units], out[:, units:]
    grad = jnp.concatenate([c[...] for c in (c0, c1, c2, c3)], axis=1)
    d_out[...] = grad
    d_inner = mx(grad, down[...], NT)
    sig = jax.nn.sigmoid(gate)
    both = gate * sig
    unit = (both * up).astype(bf)
    inner[...] = unit
    d_gate = (d_inner * up * (sig + both * (1.0 - sig))).astype(bf)
    d_up = (d_inner * both).astype(bf)
    cross[...] = row_totals(gate * d_gate.astype(jnp.float32) + up * d_up.astype(jnp.float32))
    d_low = jnp.concatenate([d_gate, d_up], axis=1)
    d_gate_up[...] = d_low
    put_blocks(mx(d_low, share[...], NT), sent, kept)
    put_blocks(mx(unit, down[...], NN), sent_down, kept_down)


def out_backward(d0, d1, d2, d3, share, gated, gain, d_normed, d_att, cross, d_mixed):
    chan = gated.shape[1]
    grad = jnp.concatenate([d[...] for d in (d0, d1, d2, d3)], axis=1)
    d_mixed[...] = grad
    out = mx(grad, share[...], NT)
    d_normed[...] = out[:, :chan]
    d_att[...] = out[:, chan:]
    cross[...] = row_totals(gated[...] * gain[...] * out[:, :chan])


def in_backward(d_shared, d_conv, d_gate, d_query, d_step, shared, conv, gate, query, step, share, d_late, cross, sent, kept):
    bf, f32 = jnp.bfloat16, jnp.float32
    steps = jnp.concatenate([d_step[...], jnp.zeros((120, TILE), f32)], axis=0).T
    low = jnp.concatenate([d_shared[...].astype(bf), d_conv[...], steps.astype(bf), d_gate[...], d_query[...]], axis=1)
    d_late[...] = jnp.concatenate([d_shared[...].astype(bf), steps.astype(bf)], axis=1)
    pairs = ((shared, d_shared), (conv, d_conv), (gate, d_gate), (query, d_query))
    products = [a[...].astype(f32) * b[...].astype(f32) for a, b in pairs]
    cross[...] = row_totals(*products) + jnp.sum(step[...] * d_step[...], axis=0, keepdims=True)
    put_blocks(mx(low, share[...], NT), sent, kept)


def call_forward(heads, held, *operands):
    conv = operands[0]
    length, chan = conv.shape
    f32, bf = jnp.float32, jnp.bfloat16
    shapes = [
        ((length, chan), f32),
        ((length, 128), bf),
        ((length, chan + 256), f32),
        ((length, chan), f32),
        ((length, 256), bf),
        ((length, 128), bf),
        ((length, 128), bf),
        ((length, 2), f32),
        ((32, length), f32),
        ((length, 8), f32),
        ((1, length), f32),
    ]
    return pl.pallas_call(
        partial(without_held, partial(mixer_forward, heads), len(operands), len(held)),
        out_shape=[jax.ShapeDtypeStruct(s, d) for s, d in shapes],
        scratch_shapes=[pltpu.VMEM((heads, length, 128), bf)],
        in_specs=[pl.BlockSpec(memory_space=pltpu.VMEM)] * len(operands)
        + [pl.BlockSpec(memory_space=pl.ANY)] * len(held),
        compiler_params=pltpu.CompilerParams(vmem_limit_bytes=VMEM_BYTES),
        cost_estimate=pl.CostEstimate(flops=3 * 10**9, bytes_accessed=16 * 10**6, transcendentals=6 * 10**6),
        name="mixer_forward",
    )(*operands, *held)


def call_backward(heads, held, *operands):
    length, chan = operands[1].shape
    f32, bf = jnp.float32, jnp.bfloat16
    shapes = [
        ((length, chan), bf),
        ((length, chan), bf),
        ((length, 128), bf),
        ((4, length, 128), f32),
        ((8, length), f32),
        ((8, chan + 256), f32),
        ((1, chan), f32),
        ((8, 128), f32),
        ((1, chan), f32),
    ]
    return pl.pallas_call(
        partial(without_held, partial(mixer_backward, heads), len(operands), len(held)),
        out_shape=[jax.ShapeDtypeStruct(s, d) for s, d in shapes],
        scratch_shapes=[
            pltpu.VMEM((length, chan), f32),
            pltpu.VMEM((length, chan), bf),
            pltpu.VMEM((heads, length, 128), bf),
            pltpu.VMEM((length, chan), f32),
        ]
        + [pltpu.VMEM((length, 128), f32) for _ in range(5)],
        in_specs=[pl.BlockSpec(memory_space=pltpu.VMEM)] * len(operands)
        + [pl.BlockSpec(memory_space=pl.ANY)] * len(held),
        compiler_params=pltpu.CompilerParams(vmem_limit_bytes=VMEM_BYTES),
        cost_estimate=pl.CostEstimate(flops=8 * 10**9, bytes_accessed=24 * 10**6, transcendentals=8 * 10**6),
        name="mixer_backward",
    )(*operands, *held)


BF = jnp.bfloat16
F32 = jnp.float32


def flip(values, axis, bits):
    size = lax.axis_size(axis)
    return lax.ppermute(values, axis, [(i, i ^ bits) for i in range(size)])


def swap(values):
    size = lax.axis_size("row")
    return lax.ppermute(
        values, ("row", "col"), [(i * size + j, j * size + i) for i in range(size) for j in range(size)]
    )


def gather_rows(values):
    far = flip(values, "row", 2)
    near = flip(values, "row", 1)
    return [values, near, far, flip(far, "row", 1)]


def total(values, axis):
    values = values + flip(values, axis, 1)
    return values + flip(values, axis, 2)


def scatter_sum(sent, kept):
    got = flip(sent, "row", 1)
    passed = (kept[1] + got[1].astype(F32)).astype(BF)
    return kept[0] + got[0].astype(F32) + flip(passed, "row", 2).astype(F32)


def tie(values, *done):
    def body(*refs):
        pass

    anywhere = pl.BlockSpec(memory_space=pl.ANY)
    return pl.pallas_call(
        body,
        out_shape=jax.ShapeDtypeStruct(values.shape, values.dtype),
        in_specs=[anywhere] * (1 + len(done)),
        out_specs=anywhere,
        input_output_aliases={0: 0},
        name="tie",
    )(values, *done)


def partner(values):
    size = lax.axis_size("dp")
    return lax.ppermute(values, "dp", [(i, i ^ 1) for i in range(size)])


def own_half(block):
    half = block.shape[0] // 2
    return lax.dynamic_slice_in_dim(block, (lax.axis_index("dp") & 1) * half, half, 0)


def fetch_halves(half):
    size = lax.axis_size("row")
    got = []
    for k in range(size):
        perm = [(i * size + j, j * size + (i ^ k)) for i in range(size) for j in range(size)]
        got.append(lax.ppermute(half, ("row", "col"), perm))
    return got, [partner(one) for one in got]


def gather_halves(half):
    got = lax.all_gather(half, "col", axis=0, tiled=False)
    row = lax.axis_index("row")
    own = [lax.dynamic_index_in_dim(got, row ^ k, 0, False) for k in range(4)]
    mine = [own[0]] + [flip(own[k], "row", k) for k in (1, 2, 3)]
    return mine, [partner(one) for one in mine], got


def split_share(grad, axis):
    return jnp.stack(jnp.split(grad.astype(BF), 4, axis=axis))


def hand_out(blocks, done=None):
    own = blocks[0] if done is None else tie(blocks[0], done)
    return jnp.stack([own] + [flip(blocks[k], "row", k) for k in (1, 2, 3)])


def send_half(blocks):
    if lax.axis_size("dp") != 2:
        return blocks, None
    half = blocks.shape[1] // 2
    bit = lax.axis_index("dp") & 1
    kept = lax.dynamic_slice_in_dim(blocks, bit * half, half, 1)
    sent = lax.dynamic_slice_in_dim(blocks, (1 - bit) * half, half, 1)
    return kept, partner(sent)


def add_half(kept, got, done=None):
    if got is None:
        return kept
    if done is not None:
        kept = tie(kept, done)
    return (kept.astype(F32) + got.astype(F32)).astype(BF)


def wait_for(values, got):
    return values if got is None else tie(values, got)


def join(half):
    if lax.axis_size("dp") != 2:
        return dp_total(half.astype(F32))
    half = half.astype(BF)
    other = partner(half)
    first = (lax.axis_index("dp") & 1) == 0
    return jnp.concatenate([jnp.where(first, half, other), jnp.where(first, other, half)], axis=0).astype(F32)


def sum_cols(blocks):
    row = lax.axis_index("row")
    ordered = jnp.stack([lax.dynamic_index_in_dim(blocks, row ^ j, 0, False) for j in range(4)])
    return lax.psum_scatter(ordered, "col", scatter_dimension=0, tiled=False)


def sum_flips(blocks):
    offset = lax.axis_index("row") ^ lax.axis_index("col")
    result = lax.dynamic_index_in_dim(blocks, offset, 0, False).astype(F32)
    for k in (1, 2, 3):
        result = result + flip(lax.dynamic_index_in_dim(blocks, offset ^ k, 0, False), "col", k).astype(F32)
    return result.astype(BF)


def dp_sum(values):
    size = lax.axis_size("dp")
    return values + partner(values) if size == 2 else lax.psum(values, "dp")


def dp_total(values):
    size = lax.axis_size("dp")
    if size == 2:
        low = values.astype(BF)
        return low.astype(F32) + lax.ppermute(low, "dp", [(0, 1), (1, 0)]).astype(F32)
    return lax.psum(values, "dp")


def t_dot(left, right):
    return lax.dot_general(left, right, (((0,), (0,)), ((), ())), preferred_element_type=F32)


def norm_back(values, scale, gain, d_normed, inner_sum, count):
    d_values = scale * (d_normed * gain[None, :]) - values * (scale * scale * scale * inner_sum / count)
    d_gain = jnp.sum(values * scale * d_normed, axis=0)
    return (d_values, d_gain)


def pad_row(values, width):
    return jnp.pad(values, (0, width - values.shape[0]))[None, :]


def shards(
    tokens,
    segments,
    cotangent,
    norm_in,
    w_gate_ssm,
    w_conv_in,
    w_step,
    w_query,
    w_shared,
    conv_main,
    conv_side,
    step_bias,
    decay_log,
    skip_gain,
    norm_ssm,
    w_ssm_out,
    w_att_out,
    norm_mlp,
    w_gate,
    w_up,
    w_down,
):
    row = lax.axis_index("row")
    length = segments.shape[1]
    heads = step_bias.shape[0]
    chan = w_gate_ssm.shape[1]
    att = w_query.shape[1]
    side = w_shared.shape[1]
    units = w_gate.shape[1]

    parts = []
    for gain in (norm_in, norm_mlp):
        for _ in range(3):
            part = lax.reduce_precision(gain, 8, 7)
            parts.append(part.astype(BF))
            gain = gain - part
    payload = jnp.concatenate([tokens, jnp.pad(jnp.stack(parts), ((0, 10), (0, 0)))], axis=0)
    x_blocks = gather_rows(payload)
    small = swap(
        jnp.concatenate(
            [
                segments.astype(F32),
                jnp.pad(
                    jnp.concatenate(
                        [
                            conv_main,
                            norm_ssm[None, :],
                            pad_row(jnp.concatenate([step_bias, decay_log, skip_gain]), chan),
                        ],
                        axis=0,
                    ),
                    ((0, 0), (0, length - chan)),
                ),
            ],
            axis=0,
        )
    )
    segment = small[0:1].astype(jnp.int32)
    conv_main = small[1:6, :chan]
    gain_ssm = small[6:7, :chan]
    step_bias, decay_log, skip_gain = (small[7, i * heads : (i + 1) * heads] for i in range(3))
    in_block = jnp.concatenate(
        [w_shared, w_conv_in, jnp.pad(w_step, ((0, 0), (0, 128 - heads))), w_gate_ssm, w_query], axis=1
    )
    in_mine, in_other = fetch_halves(own_half(in_block))
    pair_half = jnp.concatenate([own_half(jnp.concatenate([w_ssm_out, w_att_out], axis=0)), own_half(w_down)], axis=0)
    mlp_half = own_half(jnp.concatenate([w_gate, w_up], axis=1))
    pair_mine, pair_other, _ = gather_halves(tie(pair_half, x_blocks[2], *in_mine))
    mlp_mine, mlp_other, mlp_got = gather_halves(tie(mlp_half, *in_mine[:4]))
    cot_blocks = gather_rows(cotangent)
    bit = lax.axis_index("dp") & 1
    place = jnp.stack([bit, jnp.zeros_like(bit)]).astype(jnp.int32)
    place_in = jnp.stack([bit, row ^ lax.axis_index("col")]).astype(jnp.int32)

    bf, f32 = BF, F32
    weights = [(w, whole_spec(w.shape)) for w in in_mine + in_other]
    wide = 256 + 2 * chan + att
    gain_spec = pl.BlockSpec((16, 256), lambda i: (length // 16, 0))
    in_share, gains, hidden_in, scale_in, shared_own, conv_in, gate_ssm, query_in, step_in = token_call(
        project, "project", length,
        [(x, rows_spec(256)) for x in x_blocks] + [(x, gain_spec) for x in x_blocks] + weights + [(place_in, smem_spec())],
        [
            ((D, wide), bf, whole_spec((D, wide))),
            ((2, D), f32, whole_spec((2, D))),
            ((length, D), bf, rows_spec(D)),
            ((length, 1), f32, rows_spec(1)),
            ((length, side), bf, rows_spec(side)),
            ((length, chan), f32, rows_spec(chan)),
            ((length, chan), f32, rows_spec(chan)),
            ((length, att), f32, rows_spec(att)),
            ((8, length), f32, pl.BlockSpec((8, TILE), lambda i: (0, i))),
        ],
        [], 2 * length * D * wide
    )
    shared_rel = jnp.stack(gather_rows(shared_own))
    shared_abs = [lax.dynamic_index_in_dim(shared_rel, row ^ j, 0, False) for j in range(4)]
    kv_index = row * (att // HD) // (AHEADS // KVH)
    key_own = lax.dynamic_slice_in_dim(shared_abs[2], kv_index * HD, HD, 1)
    value_own = lax.dynamic_slice_in_dim(shared_abs[3], kv_index * HD, HD, 1)
    kv = jnp.concatenate([key_own, key_own, value_own, value_own], axis=1)
    state_in = jnp.concatenate(shared_abs[:2], axis=1)

    powers = jnp.arange(HD // 2).astype(F32) * (2.0 / HD)
    angles = jnp.arange(length).astype(F32)[:, None] * (rope_theta ** (-powers))[None, :]
    cosine = jnp.tile(jnp.cos(angles), (1, 4))
    sine = jnp.sin(angles)
    sine = jnp.concatenate([-sine, sine, -sine, sine], axis=1)
    seg_row = segment
    seg_col = segment.reshape(length, 1)
    taps = jnp.pad(jnp.concatenate([conv_main, conv_side], axis=1), ((0, 3), (0, 0)))
    per_head = jnp.pad(
        jnp.stack([step_bias, -jnp.exp(decay_log) * LOG2E], axis=1), ((0, 8 - heads), (0, 126))
    )
    skip = jnp.repeat(skip_gain, chan // heads)[None, :]
    gated, attended, pre, scan, bcr, qr, kk, lse, rows, dcol, square = call_forward(
        heads, [cot_blocks[3], mlp_got], conv_in, state_in, gate_ssm, query_in, kv, step_in, seg_row, seg_col, taps, per_head, skip,
        cosine, sine,
    )

    square = total(square, "row")
    half_out, half_down = (chan + att) // 2, units // 2
    out_spec = pl.BlockSpec((half_out, 256), lambda i: (0, 0))
    down_spec = pl.BlockSpec((half_down, 256), lambda i: (half_out // half_down, 0))
    weights = [(w, out_spec) for w in pair_mine + pair_other]
    deep = chan + att
    pair_out = [
        ((2, length, 256), bf, pair_spec()),
        ((2, length, 256), f32, pair_spec()),
    ]
    out_share, mix, scale_ssm, sent, kept = token_call(
        out_project, "out_project", length,
        [(gated, rows_spec(chan)), (attended, rows_spec(att)), (square, row_spec()), (gain_ssm, whole_spec((1, chan)))]
        + weights + [(place, smem_spec())],
        [
            ((deep, D), bf, whole_spec((deep, D))),
            ((length, deep), bf, rows_spec(deep)),
            ((length, 1), f32, rows_spec(1)),
        ] + pair_out,
        [], 2 * length * D * deep,
    )
    inputs = tokens.astype(F32)
    mixed = inputs + scatter_sum(sent, kept)
    mixed_blocks = gather_rows(mixed.astype(BF))

    weights = [(w, whole_spec(w.shape)) for w in mlp_mine + mlp_other]
    weights += [(w, down_spec) for w in pair_mine + pair_other]
    hidden_mlp, inner_mlp, d_gate_up, scale_mlp, cross, sent, kept, sent_down, kept_down, d_out = token_call(
        feed_forward, "feed_forward", length,
        [(m, rows_spec(256)) for m in mixed_blocks] + [(gains, whole_spec((2, D)))] + weights
        + [(c, rows_spec(256)) for c in cot_blocks] + [(place, smem_spec())],
        [
            ((length, D), bf, rows_spec(D)),
            ((length, units), bf, rows_spec(units)),
            ((length, 2 * units), bf, rows_spec(2 * units)),
            ((length, 1), f32, rows_spec(1)),
            ((1, length), f32, row_spec()),
        ] + pair_out + pair_out + [((length, D), bf, rows_spec(D))],
        [pltpu.VMEM((D, 2 * units), bf), pltpu.VMEM((units, D), bf)], 6 * length * D * 2 * units,
    )
    cross = total(cross, "row").reshape(-1, 1)
    d_hidden_mlp = scatter_sum(sent, kept)
    d_mixed_norm, grad_norm_mlp = norm_back(mixed, scale_mlp, norm_mlp, d_hidden_mlp, cross / scale_mlp, D)
    d_mixed = cotangent.astype(F32) + d_mixed_norm
    d_mixed_blocks = gather_rows(d_mixed.astype(BF))
    mlp_kept, mlp_got = send_half(split_share(t_dot(hidden_mlp, d_gate_up), 0))
    down_kept, down_got = send_half(split_share(t_dot(inner_mlp, d_out), 1))
    ready = [got for got in (mlp_got, down_got) if got is not None]
    got_down = flip(tie(sent_down, d_mixed_blocks[3]), "row", 1)
    passed_down = (kept_down[1] + got_down[1].astype(F32)).astype(BF)

    d_normed, d_att, cross, d_mixed_all = token_call(
        out_backward, "out_backward", length,
        [(d, rows_spec(256)) for d in d_mixed_blocks]
        + [(out_share, whole_spec((deep, D))), (gated, rows_spec(chan)), (gain_ssm, whole_spec((1, chan)))],
        [
            ((length, chan), f32, rows_spec(chan)),
            ((length, att), f32, rows_spec(att)),
            ((1, length), f32, row_spec()),
            ((length, D), bf, rows_spec(D)),
        ],
        [], 2 * length * D * deep, ready,
    )
    mlp_halves = add_half(mlp_kept, mlp_got, cross)
    cross = total(cross, "row")
    out_kept, out_got = send_half(split_share(t_dot(mix, d_mixed_all), 1))
    lane = jnp.arange(chan)[None, :] // (chan // heads)
    pick = (lane == jnp.arange(8)[:, None]).astype(F32)
    kv_lanes = (jnp.arange(128)[None, :] // HD == kv_index).astype(F32)
    d_gate, d_conv, d_query, d_whole, d_step, g_taps, g_skip, g_head, g_norm = call_backward(
        heads, [], d_normed, gated, scale_ssm, cross, gain_ssm, d_att, conv_in, state_in, gate_ssm, pre, scan, bcr, qr, kk,
        kv, attended, lse, rows, dcol, seg_row, seg_col, step_in, taps, per_head, skip, cosine, sine, pick, kv_lanes,
    )
    g_skip = jnp.sum(g_skip.reshape(heads, -1), axis=1)
    mlp_sum = sum_cols(hand_out(mlp_halves, d_step))
    pair_halves = jnp.concatenate([add_half(down_kept, down_got, d_step), add_half(out_kept, out_got, d_step)], axis=1)
    side_sum = total(g_taps[:5, chan:], "row")
    early = jnp.concatenate([d_conv, d_gate, d_query], axis=1)
    early_kept, early_got = send_half(split_share(t_dot(hidden_in, early), 0))
    to = [lax.dynamic_index_in_dim(d_whole, row ^ k, 0, False) for k in range(4)]
    d_shared = scatter_sum(jnp.stack([to[1].astype(BF), to[3].astype(BF)]), (to[0], to[2]))
    d_late, cross, sent, kept = token_call(
        in_backward, "in_backward", length,
        [
            (d_shared, rows_spec(side)), (d_conv, rows_spec(chan)), (d_gate, rows_spec(chan)), (d_query, rows_spec(att)),
            (d_step, pl.BlockSpec((8, TILE), lambda i: (0, i))),
            (shared_own, rows_spec(side)), (conv_in, rows_spec(chan)), (gate_ssm, rows_spec(chan)),
            (query_in, rows_spec(att)), (step_in, pl.BlockSpec((8, TILE), lambda i: (0, i))),
            (in_share, whole_spec((D, wide))),
        ],
        [((length, side + 128), bf, rows_spec(side + 128)), ((1, length), f32, row_spec())] + pair_out,
        [], 2 * length * D * wide, [side_sum],
    )
    cross = total(cross, "row")
    got = flip(wait_for(sent, early_got), "row", 1)
    passed = (kept[1] + got[1].astype(F32)).astype(BF)
    d_hidden_in = kept[0] + got[0].astype(F32) + flip(passed, "row", 2).astype(F32)
    late_halves = add_half(*send_half(split_share(t_dot(hidden_in, tie(d_late, passed)), 0)))
    early_halves = add_half(early_kept, early_got, d_hidden_in)
    grad_in = join(sum_flips(hand_out(jnp.concatenate([early_halves, late_halves], axis=2))))
    grad_early, grad_late = grad_in[:, : 2 * chan + att], grad_in[:, 2 * chan + att :]
    grad_gate_up = join(tie(mlp_sum, d_hidden_in))
    pair_sum = sum_cols(hand_out(tie(pair_halves, d_shared)))
    half_down_now = pair_sum.shape[0] * units // (units + deep)
    grad_down, grad_out = join(pair_sum[:half_down_now]), join(pair_sum[half_down_now:])
    d_inputs, grad_norm_in = norm_back(inputs, scale_in, norm_in, d_hidden_in, cross.reshape(-1, 1) / scale_in, D)
    d_tokens = d_mixed + d_inputs

    result = mixed + kept_down[0] + got_down[0].astype(F32) + flip(tie(passed_down, d_hidden_in), "row", 2).astype(F32)

    room = max(chan, conv_side.shape[1])
    by_head = jnp.concatenate(
        [
            g_taps[:5, :chan],
            g_norm,
            pad_row(jnp.concatenate([g_head[:heads, 0], g_head[:heads, 1], g_skip]), chan),
        ],
        axis=0,
    )
    by_head = swap(tie(by_head, passed))
    fields = [jnp.pad(side_sum, ((0, 0), (0, room - conv_side.shape[1])))]
    fields.append(pad_row(grad_norm_mlp, room))
    fields.append(pad_row(grad_norm_in, room))
    by_head = total(by_head, "row")
    sums = total(jnp.concatenate(fields, axis=0), "col")
    sums = dp_sum(jnp.concatenate([jnp.pad(by_head, ((0, 0), (0, room - chan))), sums], axis=0))
    by_head = sums[:7]
    grad_side = sums[7:12]
    return (
        result.astype(BF),
        d_tokens,
        sums[13, : norm_in.shape[0]],
        grad_early[:, chan : 2 * chan],
        grad_early[:, :chan],
        grad_late[:, side : side + heads],
        grad_early[:, 2 * chan :],
        grad_late[:, :side],
        by_head[:5, :chan],
        grad_side[:, : conv_side.shape[1]],
        by_head[6, :heads],
        by_head[6, heads : 2 * heads],
        by_head[6, 2 * heads : 3 * heads],
        by_head[5, :chan],
        grad_out[:chan],
        grad_out[chan:],
        sums[12, : norm_mlp.shape[0]],
        grad_gate_up[:, :units],
        grad_gate_up[:, units:],
        grad_down,
    )


def solution(mesh):
    return jax.shard_map(
        shards,
        mesh=mesh,
        in_specs=(
            P(("dp", "col"), "row"),
            P(("dp", "row"), None),
            P(("dp", "col"), "row"),
            P("row"),
            P("row", "col"),
            P("row", "col"),
            P("row", "col"),
            P("row", "col"),
            P("row", "col"),
            P(None, "col"),
            P(),
            P("col"),
            P("col"),
            P("col"),
            P("col"),
            P("col", "row"),
            P("col", "row"),
            P("row"),
            P("row", "col"),
            P("row", "col"),
            P("col", "row"),
        ),
        out_specs=(
            P(("dp", "col"), "row"),
            P(("dp", "col"), "row"),
            P("row"),
            P("row", "col"),
            P("row", "col"),
            P("row", "col"),
            P("row", "col"),
            P("row", "col"),
            P(None, "col"),
            P(),
            P("col"),
            P("col"),
            P("col"),
            P("col"),
            P("col", "row"),
            P("col", "row"),
            P("row"),
            P("row", "col"),
            P("row", "col"),
            P("col", "row"),
        ),
        check_vma=False,
    )
```
